128 devices in a mesh: occ: 8 (over y, core), va: 2 (over z_lo), vb: 8 (over x, z_hi).
Axes of the slice: x: 4, y: 4, z: 4 (z_hi: 2, z_lo: 2; z = z_hi * 2 + z_lo), core: 2. Of those that a mesh axis runs over, the one named last changes fastest.
Arguments:
- factors: float32 [24, 1024, 1408], P('occ', ('va', 'vb')), may hold values from -0.04 to 0.04
- eps_occ: float32 [24], P('occ'), may hold values from -2 to -0.4
- eps_vir: float32 [1024], P(('va', 'vb')), may hold values from 0.2 to 3
Outputs:
- pair_energy: float32 [24, 24], P('occ')
The draws below stay inside these ranges and needn't reach their ends.
All inputs are finite; a program needn't handle non-finite values.
Results may differ from the reference program's by a relative error of at most 0.00007.
Values sent between devices are 32-bit elements; how exact they have to be, the bound alone decides.
A program may use at most 128 MiB of HBM per device.

```python
import jax
import jax.numpy as jnp
from jax import lax

V = 1024
NAUX = 1408
O = 24


def draw_factors(key, part):
    key = jax.random.fold_in(key, 7)
    shared_key, own_key = jax.random.split(key)
    shared = jax.random.truncated_normal(shared_key, -4.0, 4.0, (V, NAUX), jnp.float32)
    own = jax.random.truncated_normal(own_key, -4.0, 4.0, (O, V, NAUX), jnp.float32)
    return (0.005 * (shared[None, :, :] + own)).astype(jnp.float32)


def shard_levels(key, shape, pieces, least, high):
    factor_of, own = 1.0, jax.random.fold_in(key, 6)
    for axis_at, blocks in pieces:
        steps = jnp.exp(jax.random.uniform(jax.random.fold_in(own, axis_at), (blocks,), jnp.float32, least / len(pieces), high / len(pieces)))
        factor_of = factor_of * jnp.repeat(steps, shape[axis_at] // blocks).reshape([-1 if axis == axis_at else 1 for axis in range(len(shape))])
    return factor_of


def setup_inputs(seed: int = 0) -> dict:
    arg_keys = jax.random.split(jax.random.key(seed), 4)
    return {
        "factors": draw_factors(jax.random.fold_in(arg_keys[3], 71), 0),
        "eps_occ": jnp.clip(-2.0 + 1.6 * jax.random.uniform(arg_keys[1], (O,), jnp.float32) ** shard_levels(arg_keys[1], (O,), ((0, 8),), -0.2, 0.2), -2.0, -0.4),
        "eps_vir": jnp.clip(0.2 + 2.8 * jax.random.uniform(arg_keys[2], (V,), jnp.float32) ** shard_levels(arg_keys[2], (V,), ((0, 16),), -0.2, 0.2), 0.2, 3.0),
    }


def reference(factors, eps_occ, eps_vir):
    def one_pair_row(index):
        left = lax.dynamic_index_in_dim(factors, index, 0, keepdims=False)
        direct = jnp.einsum("ap,jbp->jab", left, factors, precision=lax.Precision.HIGHEST)
        swapped = jnp.transpose(direct, (0, 2, 1))
        eps_here = lax.dynamic_index_in_dim(eps_occ, index, 0, keepdims=False)
        denom = eps_vir[None, :, None] + eps_vir[None, None, :] - eps_here - eps_occ[:, None, None]
        return -jnp.sum(direct * (2.0 * direct - swapped) / denom, axis=(1, 2))

    return lax.map(one_pair_row, jnp.arange(factors.shape[0], dtype=jnp.int32))
```

```python
import functools

import jax
import jax.numpy as jnp
from jax import lax
from jax.experimental import pallas as pl
from jax.experimental.pallas import tpu as pltpu
from jax.sharding import PartitionSpec as P

MESH = pl.DeviceIdType.MESH
STEPS = ((1, 0, 0), (3, 0, 0), (0, 1, 0), (0, 3, 0), (0, 0, 1), (0, 0, 3))
OCC, SUB, NAUX = 24, 16, 1408
ROWS = OCC * SUB

POINTS = ((0, 0, 0), (0, 0, 1), (1, 0, 0), (3, 0, 0), (0, 1, 1), (1, 3, 0), (1, 0, 3), (0, 0, 3), (1, 3, 1), (3, 1, 1), (2, 0, 3), (0, 2, 1))
HOPS = (
    (0, 0, -1, -1),
    (0, 1, -1, -1),
    (0, 3, -1, -1),
    (1, 0, 4, 0),
    (2, 0, 0, 0),
    (3, 0, 1, 0),
    (7, 0, 5, 0),
    (0, 2, -1, -1),
    (1, 3, 4, 0),
    (2, 3, 0, 0),
    (3, 3, 1, 0),
    (7, 3, 5, 0),
    (4, 0, 2, 1),
    (5, 0, 3, 2),
    (1, 1, 4, 0),
    (2, 1, 0, 0),
    (3, 1, 1, 0),
    (6, 0, 5, 2),
    (4, 3, 2, 1),
    (5, 3, 3, 2),
    (1, 2, 4, 0),
    (2, 2, 0, 0),
    (3, 2, 1, 0),
    (7, 2, 5, 0),
    (4, 1, 2, 1),
    (5, 1, 3, 2),
    (6, 1, 5, 2),
    (6, 3, 0, 7),
    (8, 0, 4, 5),
    (9, 0, 1, 4),
    (4, 2, 2, 1),
    (5, 2, 3, 2),
    (6, 2, 5, 2),
    (8, 3, 4, 5),
    (9, 3, 1, 4),
    (10, 0, 0, 6),
    (11, 0, 2, 4),
    (7, 1, 5, 0),
    (8, 1, 4, 5),
    (9, 1, 1, 4),
    (10, 1, 0, 6),
    (11, 3, 2, 4),
    (8, 2, 4, 5),
    (9, 2, 1, 4),
    (10, 2, 0, 6),
    (11, 1, 2, 4),
    (10, 3, 0, 6),
    (11, 2, 2, 4),
)
UPTO = (24, 24, 24, 36, 36, 36, 37, 41, 41, 41, 45, 45, 45, 47, 48, 48, 48, 48)
UNITS = (
    ((0, 0, 1), (0, 1, 2)),
    ((0, 2, 2), (1, 2, 2)),
    ((1, 3, 2), (2, 3, 1)),
    ((0, 4, 2), (1, 4, 2)),
    ((4, 3, 2), (0, 5, 2)),
    ((1, 5, 2), (4, 5, 2)),
    ((5, 3, 2), (6, 3, 2)),
    ((1, 6, 2), (4, 6, 2)),
    ((6, 5, 2), (7, 5, 2)),
    ((1, 7, 1), (7, 4, 2)),
    ((4, 8, 2), (8, 3, 2)),
    ((6, 9, 2), (2, 9, 2)),
    ((5, 9, 2), (8, 9, 1)),
    ((1, 10, 1), (5, 10, 2)),
    ((8, 10, 2), (0, 11, 2)),
    ((1, 11, 1), (7, 11, 1)),
    ((11, 6, 2), (11, 8, 2)),
    ((11, 10, 1), (11, 3, 2)),
)

SLOTS = len(POINTS)
CHILDREN = {}
for _slot, _part, _way, _from in HOPS:
    if _way >= 0:
        CHILDREN.setdefault((_from, _part), []).append((_slot, _way))
EPS_FROM = {slot: (source, way) for slot, part, way, source in HOPS if part == 0 and way >= 0}
READY = []
_seen = set()
for _pair in UNITS:
    _new = sorted({slot for unit in _pair for slot in unit[:2]} - _seen)
    _seen.update(_new)
    READY.append(_new)


def pick(step, core, field):
    value = jnp.int32(0)
    for index, pair in enumerate(UNITS):
        for side in range(2):
            if pair[side][field]:
                hit = (step == index) & (core == side)
                value = jnp.where(hit, jnp.int32(pair[side][field]), value)
    return value


def swap_pairs(rows, lane):
    rows = list(rows)
    for bit in (4, 2, 1):
        low = (lane // (16 * bit)) % 2 == 0
        for r in range(8):
            if r & bit:
                continue
            first, second = rows[r], rows[r + bit]
            rows[r] = jnp.where(low, first, pltpu.roll(second, 16 * bit, 1))
            rows[r + bit] = jnp.where(low, pltpu.roll(first, 128 - 16 * bit, 1), second)
    return rows


def kernel(
    eps_occ, eps_vir, b_ref, out_ref,
    held, high, low, tile, acc, evs, eo_block, eo_lane,
    hop_out, hop_in, sib_out, sib_in, row_out, row_in, ev_out, ev_in, eo_out, eo_in, own_sem,
):
    occ, va, vb = lax.axis_index("occ"), lax.axis_index("va"), lax.axis_index("vb")
    y, core = occ // 2, occ % 2
    x, z = vb // 2, (vb % 2) * 2 + va
    other = 1 - core

    def device(cx, cy, cz, ck):
        return (cy * 2 + ck, cz % 2, cx * 2 + cz // 2)

    sibling = device(x, y, z, other)

    def to_step(way):
        dx, dy, dz = STEPS[way]
        return device((x + 4 - dx) % 4, (y + 4 - dy) % 4, (z + 4 - dz) % 4, core)

    line = [(dy, dk) for dy in range(4) for dk in range(2) if (dy, dk) != (0, 0)]

    def line_device(dy, dk):
        return device(x, (y + dy) % 4, z, other if dk else core)

    barrier = pltpu.get_barrier_semaphore()
    partners = [to_step(way) for way in (0, 1, 4, 5)] + [line_device(dy, dk) for dy, dk in line]
    for partner in partners:
        pl.semaphore_signal(barrier, inc=1, device_id=partner, device_id_type=MESH)
    pl.semaphore_wait(barrier, len(partners))

    def piece(slot, part, half):
        start = ((y + POINTS[slot][1] + part) % 4) * 6
        return held.at[slot, pl.ds(start, 6), pl.ds(pl.multiple_of(half * 8, 8), 8), :]

    def row_copy(dy, dk):
        far = line_device(dy, dk)
        far_occ = far[0]
        return pltpu.make_async_remote_copy(
            src_ref=b_ref.at[:, pl.ds(pl.multiple_of(far_occ * 8, 8), 8), :],
            dst_ref=held.at[0, pl.ds(occ * 3, 3), pl.ds(pl.multiple_of((far_occ % 2) * 8, 8), 8), :],
            send_sem=row_out.at[dy, dk], recv_sem=row_in.at[dy, dk],
            device_id=far, device_id_type=MESH,
        )

    def row_arrival(dy, dk):
        near = line_device((4 - dy) % 4, dk)
        place = held.at[0, pl.ds(near[0] * 3, 3), pl.ds(pl.multiple_of(core * 8, 8), 8), :]
        return pltpu.make_async_remote_copy(
            src_ref=place, dst_ref=place, send_sem=row_out.at[dy, dk], recv_sem=row_in.at[dy, dk],
            device_id=near, device_id_type=MESH,
        )

    def sib_copy(slot, part):
        return pltpu.make_async_remote_copy(
            src_ref=piece(slot, part, core), dst_ref=piece(slot, part, core),
            send_sem=sib_out.at[slot, part], recv_sem=sib_in.at[slot, part],
            device_id=sibling, device_id_type=MESH,
        )

    def sib_arrival(slot, part):
        return pltpu.make_async_remote_copy(
            src_ref=piece(slot, part, other), dst_ref=piece(slot, part, other),
            send_sem=sib_out.at[slot, part], recv_sem=sib_in.at[slot, part],
            device_id=sibling, device_id_type=MESH,
        )

    def hop_copy(slot, part, way, source):
        return pltpu.make_async_remote_copy(
            src_ref=piece(source, part, core),
            dst_ref=held.at[
                slot,
                pl.ds(((y + POINTS[source][1] + part) % 4) * 6, 6),
                pl.ds(pl.multiple_of(core * 8, 8), 8),
                :,
            ],
            send_sem=hop_out.at[slot, part], recv_sem=hop_in.at[slot, part],
            device_id=to_step(way), device_id_type=MESH,
        )

    def hop_arrival(slot, part, way):
        return pltpu.make_async_remote_copy(
            src_ref=piece(slot, part, core), dst_ref=piece(slot, part, core),
            send_sem=hop_out.at[slot, part], recv_sem=hop_in.at[slot, part],
            device_id=to_step(way), device_id_type=MESH,
        )

    def ev_copy(slot, way, source):
        return pltpu.make_async_remote_copy(
            src_ref=evs.at[source], dst_ref=evs.at[slot], send_sem=ev_out.at[slot], recv_sem=ev_in.at[slot],
            device_id=to_step(way), device_id_type=MESH,
        )

    def eo_copy(dy, dk):
        return pltpu.make_async_remote_copy(
            src_ref=eo_block.at[pl.ds(occ * 3, 3)], dst_ref=eo_block.at[pl.ds(occ * 3, 3)],
            send_sem=eo_out.at[dy, dk], recv_sem=eo_in.at[dy, dk],
            device_id=line_device(dy, dk), device_id_type=MESH,
        )

    def eo_arrival(dy, dk):
        near = line_device((4 - dy) % 4, dk)
        place = eo_block.at[pl.ds(near[0] * 3, 3)]
        return pltpu.make_async_remote_copy(
            src_ref=place, dst_ref=place, send_sem=eo_out.at[dy, dk], recv_sem=eo_in.at[dy, dk],
            device_id=near, device_id_type=MESH,
        )

    own = pltpu.make_async_copy(
        b_ref.at[:, pl.ds(pl.multiple_of(occ * 8, 8), 8), :],
        held.at[0, pl.ds(occ * 3, 3), pl.ds(pl.multiple_of(core * 8, 8), 8), :],
        own_sem,
    )
    row_copy(0, 1).start()
    own.start()
    for dy, dk in line[1:]:
        if dy != 2:
            row_copy(dy, dk).start()
    for dk in range(2):
        row_copy(2, dk).start()

    lane = lax.broadcasted_iota(jnp.int32, (8, 128), 1)
    sub16 = lax.broadcasted_iota(jnp.int32, (16, 128), 0)
    down = jnp.zeros((16, 128), jnp.float32)
    across = jnp.zeros((8, 128), jnp.float32)
    for a in range(SUB):
        value = eps_vir[y * SUB + a]
        down = jnp.where(sub16 == a, value, down)
        across = jnp.where(lane % SUB == a, value, across)
    evs[0, :16, :] = down
    evs[0, 16:, :] = across
    for r in range(3):
        eo_block[occ * 3 + r] = jnp.full((8, 128), eps_occ[r], jnp.float32)
    for slot, (source, way) in EPS_FROM.items():
        if source == 0:
            ev_copy(slot, way, source).start()
    for dy, dk in line:
        eo_copy(dy, dk).start()
    acc[...] = jnp.zeros_like(acc)

    def event(slot, part, way):
        if slot == 0:
            dy = (4 - part) % 4
            for dk in range(2):
                if (dy, dk) == (0, 0):
                    own.wait()
                else:
                    row_arrival(dy, dk).wait_recv()
        else:
            hop_arrival(slot, part, way).wait_recv()
        for child, child_way in CHILDREN.get((slot, part), []):
            hop_copy(child, part, child_way, slot).start()
        sib_copy(slot, part).start()
        if part == 0 and slot:
            source, ev_way = EPS_FROM[slot]
            ev_copy(slot, ev_way, source).wait_recv()
            for child, (child_from, child_way) in EPS_FROM.items():
                if child_from == slot:
                    ev_copy(child, child_way, slot).start()

    def split(slot):
        def rows(i, carry):
            value = held[slot, i]
            top = value.astype(jnp.bfloat16)
            at = pl.ds(pl.multiple_of(i * SUB, SUB), SUB)
            high[slot, at, :] = top
            low[slot, at, :] = (value - top.astype(jnp.float32)).astype(jnp.bfloat16)
            return carry
        lax.fori_loop(0, OCC, rows, 0)

    contract = (((1,), (1,)), ((), ()))

    def step_body(step, split_done):
        split_upto = jnp.int32(0)
        total = 0
        for index in range(len(UNITS)):
            first = 0 if index == 0 else UPTO[index - 1]

            @pl.when(step == index)
            def _():
                for slot, part, way, _source in HOPS[first:UPTO[index]]:
                    event(slot, part, way)
                for slot in READY[index]:
                    for part in range(4):
                        sib_arrival(slot, part).wait_recv()
                if index == 0:
                    for dy, dk in line:
                        eo_arrival(dy, dk).wait_recv()
                    for block in range(3):
                        value = jnp.zeros((8, 128), jnp.float32)
                        for r in range(8):
                            value = jnp.where(lane // SUB == r, eo_block[block * 8 + r], value)
                        eo_lane[block] = value

            total += len(READY[index])
            split_upto = jnp.where(step == index, jnp.int32(total), split_upto)

        def one_split(index, carry):
            split(index)
            return carry

        lax.fori_loop(split_done, split_upto, one_split, 0)

        left, right = pick(step, core, 0), pick(step, core, 1)
        weight = pick(step, core, 2)
        scale = jnp.where(weight == 2, jnp.float32(0.5), jnp.float32(1.0))

        lh, ll, rh, rl = high[left], low[left], high[right], low[right]
        dot = functools.partial(lax.dot_general, dimension_numbers=contract, preferred_element_type=jnp.float32)
        tile[...] = dot(lh, rl) + dot(ll, rh) + dot(lh, rh)

        down = evs[left, :16, :] * scale
        across = evs[right, 16:, :]
        for block_j in range(3):
            lanes = pl.ds(block_j * 128, 128)
            row = across - eo_lane[block_j]
            for block_i in range(block_j + 1):
                mirror = swap_pairs(
                    [tile[(block_j * 8 + r) * SUB:(block_j * 8 + r + 1) * SUB, block_i * 128:block_i * 128 + 128] for r in range(8)],
                    lax.broadcasted_iota(jnp.int32, (SUB, 128), 1),
                )
                for r in range(8):
                    i = block_i * 8 + r
                    here = tile[i * SUB:(i + 1) * SUB, lanes]
                    shift = (row - eo_block[i]) * scale
                    denom = down + jnp.concatenate([shift, shift], axis=0)
                    guess = pl.reciprocal(denom, approx=True)
                    inverse = guess * (2.0 - denom * guess)
                    term = (here * (here - mirror[r]) + mirror[r] * mirror[r]) * inverse
                    acc[i, :, lanes] = acc[i, :, lanes] + (term[:8] + term[8:])
        return split_upto

    lax.fori_loop(0, len(UNITS), step_body, jnp.int32(0))

    group = (lax.broadcasted_iota(jnp.int32, (ROWS, 128), 0) // SUB == lax.broadcasted_iota(jnp.int32, (ROWS, 128), 1)).astype(jnp.float32)
    sums = lax.dot_general(
        jnp.sum(acc[...], axis=1), group, (((1,), (0,)), ((), ())),
        precision=lax.Precision.HIGHEST, preferred_element_type=jnp.float32,
    )
    out_ref[...] = -sums

    for dy, dk in line:
        row_copy(dy, dk).wait_send()
        eo_copy(dy, dk).wait_send()
    for slot, part, way, source in HOPS:
        sib_copy(slot, part).wait_send()
        if way >= 0:
            hop_copy(slot, part, way, source).wait_send()
    for slot, (source, way) in EPS_FROM.items():
        ev_copy(slot, way, source).wait_send()


def on_device(factors, eps_occ, eps_vir):
    f32, dma = jnp.float32, pltpu.SemaphoreType.DMA
    part = pl.pallas_call(
        kernel,
        out_shape=jax.ShapeDtypeStruct((OCC, 128), f32),
        in_specs=[
            pl.BlockSpec(memory_space=pltpu.SMEM),
            pl.BlockSpec(memory_space=pltpu.SMEM),
            pl.BlockSpec(memory_space=pltpu.VMEM),
        ],
        out_specs=pl.BlockSpec(memory_space=pltpu.VMEM),
        scratch_shapes=[
            pltpu.VMEM((SLOTS, OCC, SUB, NAUX), f32),
            pltpu.VMEM((SLOTS, ROWS, NAUX), jnp.bfloat16),
            pltpu.VMEM((SLOTS, ROWS, NAUX), jnp.bfloat16),
            pltpu.VMEM((ROWS, ROWS), f32),
            pltpu.VMEM((OCC, 8, ROWS), f32),
            pltpu.VMEM((SLOTS, 24, 128), f32),
            pltpu.VMEM((OCC, 8, 128), f32),
            pltpu.VMEM((3, 8, 128), f32),
            dma((SLOTS, 4)), dma((SLOTS, 4)),
            dma((SLOTS, 4)), dma((SLOTS, 4)),
            dma((4, 2)), dma((4, 2)),
            dma((SLOTS,)), dma((SLOTS,)),
            dma((4, 2)), dma((4, 2)),
            dma,
        ],
        compiler_params=pltpu.CompilerParams(
            collective_id=0, has_side_effects=True, vmem_limit_bytes=61 * 2**20
        ),
        cost_estimate=pl.CostEstimate(flops=45 * 10**9, bytes_accessed=2 * 10**6, transcendentals=0),
    )(eps_occ, eps_vir, factors)
    total = lax.psum(part[:, :OCC], ("occ", "va", "vb"))
    block = jnp.arange(OCC) // 8
    total = total + jnp.where(block[:, None] > block[None, :], total.T, 0.0)
    return lax.dynamic_slice_in_dim(total, lax.axis_index("occ") * 3, 3, 0)


def solution(mesh):
    placed = (P("occ", ("va", "vb"), None), P("occ"), P(("va", "vb")))
    return jax.shard_map(on_device, mesh=mesh, in_specs=placed, out_specs=P("occ", None), check_vma=False)
```

```python
import functools

import jax
import jax.numpy as jnp
from jax import lax
from jax.experimental import pallas as pl
from jax.experimental.pallas import tpu as pltpu
from jax.sharding import PartitionSpec as P

MESH = pl.DeviceIdType.MESH
STEPS = ((1, 0, 0), (3, 0, 0), (0, 1, 0), (0, 3, 0), (0, 0, 1), (0, 0, 3))
OCC, SUB, NAUX = 24, 16, 1408
ROWS = OCC * SUB

POINTS = ((0, 0, 0), (0, 0, 1), (1, 0, 0), (0, 0, 3), (3, 0, 1), (0, 1, 0), (1, 3, 0), (0, 0, 2), (2, 3, 0), (3, 0, 2), (0, 2, 0), (2, 2, 0))
HOPS = (
    (0, 0, -1, -1),
    (0, 1, -1, -1),
    (0, 3, -1, -1),
    (1, 0, 4, 0),
    (3, 0, 5, 0),
    (2, 0, 0, 0),
    (0, 2, -1, -1),
    (1, 1, 4, 0),
    (3, 1, 5, 0),
    (2, 1, 0, 0),
    (4, 0, 1, 1),
    (5, 0, 2, 0),
    (6, 0, 3, 2),
    (1, 3, 4, 0),
    (3, 3, 5, 0),
    (2, 3, 0, 0),
    (4, 1, 1, 1),
    (5, 1, 2, 0),
    (6, 1, 3, 2),
    (1, 2, 4, 0),
    (7, 0, 5, 3),
    (2, 2, 0, 0),
    (4, 3, 1, 1),
    (5, 3, 2, 0),
    (6, 3, 3, 2),
    (3, 2, 5, 0),
    (8, 0, 0, 6),
    (9, 0, 4, 4),
    (4, 2, 1, 1),
    (5, 2, 2, 0),
    (6, 2, 3, 2),
    (7, 1, 5, 3),
    (7, 3, 4, 1),
    (8, 1, 0, 6),
    (10, 0, 2, 5),
    (11, 0, 3, 8),
    (7, 2, 4, 1),
    (8, 3, 0, 6),
    (9, 1, 1, 7),
    (10, 1, 2, 5),
    (11, 1, 3, 8),
    (8, 2, 0, 6),
    (9, 2, 4, 4),
    (9, 3, 1, 7),
    (10, 3, 2, 5),
    (11, 3, 3, 8),
    (10, 2, 2, 5),
    (11, 2, 3, 8),
)
UPTO = (
    23, 23, 23, 28, 29, 29, 29, 34, 34, 34, 34, 36,
    38, 39, 39, 39, 41, 43, 44, 44, 46, 46, 46, 46,
    46, 48, 48, 48, 48, 48, 48, 48, 48, 48, 48, 48,
)
UNITS = (
    ((0, 0, 1), (1, 0, 2)),
    ((0, 2, 2), (2, 1, 2)),
    ((3, 1, 1), (2, 3, 2)),
    ((2, 4, 2), (4, 3, 2)),
    ((0, 5, 2), (2, 5, 2)),
    ((5, 1, 2), (5, 4, 2)),
    ((5, 3, 2), (1, 6, 2)),
    ((3, 6, 2), (6, 5, 2)),
    ((4, 6, 2), (6, 7, 2)),
    ((7, 5, 2), (8, 0, 2)),
    ((5, 8, 1), (8, 7, 2)),
    ((8, 3, 2), (8, 4, 2)),
    ((5, 9, 2), (9, 2, 1)),
    ((1, 10, 2), (10, 7, 1)),
    ((9, 10, 2), (6, 10, 2)),
    ((10, 4, 2), (0, 10, 1)),
    ((4, 11, 2), (7, 11, 1)),
    ((10, 11, 1), (1, 11, 2)),
)

SLOTS = len(POINTS)
CHILDREN = {}
for _slot, _part, _way, _from in HOPS:
    if _way >= 0:
        CHILDREN.setdefault((_from, _part), []).append((_slot, _way))
EPS_FROM = {slot: (source, way) for slot, part, way, source in HOPS if part == 0 and way >= 0}
READY = []
_seen = set()
for _pair in UNITS:
    _new = sorted({slot for unit in _pair for slot in unit[:2]} - _seen)
    _seen.update(_new)
    READY.append(_new)


def pick(step, core, field):
    value = jnp.int32(0)
    for index, pair in enumerate(UNITS):
        for side in range(2):
            if pair[side][field]:
                hit = (step == index) & (core == side)
                value = jnp.where(hit, jnp.int32(pair[side][field]), value)
    return value


def swap_pairs(rows, lane):
    rows = list(rows)
    for bit in (4, 2, 1):
        low = (lane // (16 * bit)) % 2 == 0
        for r in range(8):
            if r & bit:
                continue
            first, second = rows[r], rows[r + bit]
            rows[r] = jnp.where(low, first, pltpu.roll(second, 16 * bit, 1))
            rows[r + bit] = jnp.where(low, pltpu.roll(first, 128 - 16 * bit, 1), second)
    return rows


def kernel(
    eps_occ, eps_vir, b_ref, out_ref,
    held, both, tile, acc, evs, eo_block, eo_lane,
    rows_out, rows_got, x_got, z_got,
    hop_out, hop_in, sib_out, sib_in, row_out, row_in, ev_out, ev_in, eo_out, eo_in, own_sem,
    red_out, red_in, plane_out, plane_in,
):
    occ, va, vb = lax.axis_index("occ"), lax.axis_index("va"), lax.axis_index("vb")
    y, core = occ // 2, occ % 2
    x, z = vb // 2, (vb % 2) * 2 + va
    other = 1 - core

    def device(cx, cy, cz, ck):
        return (cy * 2 + ck, cz % 2, cx * 2 + cz // 2)

    sibling = device(x, y, z, other)

    def to_step(way):
        dx, dy, dz = STEPS[way]
        return device((x + 4 - dx) % 4, (y + 4 - dy) % 4, (z + 4 - dz) % 4, core)

    line = [(dy, dk) for dy in range(4) for dk in range(2) if (dy, dk) != (0, 0)]

    def line_device(dy, dk):
        return device(x, (y + dy) % 4, z, other if dk else core)

    barrier = pltpu.get_barrier_semaphore()
    partners = [line_device(dy, dk) for dy, dk in line]
    partners += [device((x + d) % 4, y, z, core) for d in range(1, 4)]
    partners += [device(x, y, (z + d) % 4, core) for d in range(1, 4)]
    for partner in partners:
        pl.semaphore_signal(barrier, inc=1, device_id=partner, device_id_type=MESH)
    pl.semaphore_wait(barrier, len(partners))

    def piece(slot, part, half):
        start = ((y + POINTS[slot][1] + part) % 4) * 6
        return held.at[slot, pl.ds(start, 6), pl.ds(pl.multiple_of(half * 8, 8), 8), :]

    def row_copy(dy, dk):
        far = line_device(dy, dk)
        far_occ = far[0]
        return pltpu.make_async_remote_copy(
            src_ref=b_ref.at[:, pl.ds(pl.multiple_of(far_occ * 8, 8), 8), :],
            dst_ref=held.at[0, pl.ds(occ * 3, 3), pl.ds(pl.multiple_of((far_occ % 2) * 8, 8), 8), :],
            send_sem=row_out.at[dy, dk], recv_sem=row_in.at[dy, dk],
            device_id=far, device_id_type=MESH,
        )

    def row_arrival(dy, dk):
        near = line_device((4 - dy) % 4, dk)
        place = held.at[0, pl.ds(near[0] * 3, 3), pl.ds(pl.multiple_of(core * 8, 8), 8), :]
        return pltpu.make_async_remote_copy(
            src_ref=place, dst_ref=place, send_sem=row_out.at[dy, dk], recv_sem=row_in.at[dy, dk],
            device_id=near, device_id_type=MESH,
        )

    def sib_copy(slot, part):
        return pltpu.make_async_remote_copy(
            src_ref=piece(slot, part, core), dst_ref=piece(slot, part, core),
            send_sem=sib_out.at[slot, part], recv_sem=sib_in.at[slot, part],
            device_id=sibling, device_id_type=MESH,
        )

    def sib_arrival(slot, part):
        return pltpu.make_async_remote_copy(
            src_ref=piece(slot, part, other), dst_ref=piece(slot, part, other),
            send_sem=sib_out.at[slot, part], recv_sem=sib_in.at[slot, part],
            device_id=sibling, device_id_type=MESH,
        )

    def hop_copy(slot, part, way, source):
        return pltpu.make_async_remote_copy(
            src_ref=piece(source, part, core),
            dst_ref=held.at[
                slot,
                pl.ds(((y + POINTS[source][1] + part) % 4) * 6, 6),
                pl.ds(pl.multiple_of(core * 8, 8), 8),
                :,
            ],
            send_sem=hop_out.at[slot, part], recv_sem=hop_in.at[slot, part],
            device_id=to_step(way), device_id_type=MESH,
        )

    def hop_arrival(slot, part, way):
        return pltpu.make_async_remote_copy(
            src_ref=piece(slot, part, core), dst_ref=piece(slot, part, core),
            send_sem=hop_out.at[slot, part], recv_sem=hop_in.at[slot, part],
            device_id=to_step(way), device_id_type=MESH,
        )

    def ev_copy(slot, way, source):
        return pltpu.make_async_remote_copy(
            src_ref=evs.at[source], dst_ref=evs.at[slot], send_sem=ev_out.at[slot], recv_sem=ev_in.at[slot],
            device_id=to_step(way), device_id_type=MESH,
        )

    def eo_copy(dy, dk):
        return pltpu.make_async_remote_copy(
            src_ref=eo_block.at[pl.ds(occ * 3, 3)], dst_ref=eo_block.at[pl.ds(occ * 3, 3)],
            send_sem=eo_out.at[dy, dk], recv_sem=eo_in.at[dy, dk],
            device_id=line_device(dy, dk), device_id_type=MESH,
        )

    def eo_arrival(dy, dk):
        near = line_device((4 - dy) % 4, dk)
        place = eo_block.at[pl.ds(near[0] * 3, 3)]
        return pltpu.make_async_remote_copy(
            src_ref=place, dst_ref=place, send_sem=eo_out.at[dy, dk], recv_sem=eo_in.at[dy, dk],
            device_id=near, device_id_type=MESH,
        )

    own = pltpu.make_async_copy(
        b_ref.at[:, pl.ds(pl.multiple_of(occ * 8, 8), 8), :],
        held.at[0, pl.ds(occ * 3, 3), pl.ds(pl.multiple_of(core * 8, 8), 8), :],
        own_sem,
    )
    row_copy(0, 1).start()
    own.start()
    for dy, dk in line[1:]:
        if dy != 2:
            row_copy(dy, dk).start()
    for dk in range(2):
        row_copy(2, dk).start()

    lane = lax.broadcasted_iota(jnp.int32, (8, 128), 1)
    sub16 = lax.broadcasted_iota(jnp.int32, (16, 128), 0)
    down = jnp.zeros((16, 128), jnp.float32)
    across = jnp.zeros((8, 128), jnp.float32)
    for a in range(SUB):
        value = eps_vir[y * SUB + a]
        down = jnp.where(sub16 == a, value, down)
        across = jnp.where(lane % SUB == a, value, across)
    evs[0, :16, :] = down
    evs[0, 16:, :] = across
    for r in range(3):
        eo_block[occ * 3 + r] = jnp.full((8, 128), eps_occ[r], jnp.float32)
    for slot, (source, way) in EPS_FROM.items():
        if source == 0:
            ev_copy(slot, way, source).start()
    for dy, dk in line:
        eo_copy(dy, dk).start()
    acc[...] = jnp.zeros_like(acc)

    def event(slot, part, way):
        if slot == 0:
            dy = (4 - part) % 4
            for dk in range(2):
                if (dy, dk) == (0, 0):
                    own.wait()
                else:
                    row_arrival(dy, dk).wait_recv()
        else:
            hop_arrival(slot, part, way).wait_recv()
        for child, child_way in CHILDREN.get((slot, part), []):
            hop_copy(child, part, child_way, slot).start()
        sib_copy(slot, part).start()
        if part == 0 and slot:
            source, ev_way = EPS_FROM[slot]
            ev_copy(slot, ev_way, source).wait_recv()
            for child, (child_from, child_way) in EPS_FROM.items():
                if child_from == slot:
                    ev_copy(child, child_way, slot).start()

    def split(slot):
        def rows(i, carry):
            value = held[slot, i]
            top = value.astype(jnp.bfloat16)
            at = pl.ds(pl.multiple_of(i * SUB, SUB), SUB)
            both[slot, at, :] = top
            both[slot, pl.ds(pl.multiple_of(ROWS + i * SUB, SUB), SUB), :] = (value - top.astype(jnp.float32)).astype(jnp.bfloat16)
            return carry
        lax.fori_loop(0, OCC, rows, 0)

    contract = (((1,), (1,)), ((), ()))

    def step_body(step, split_done):
        split_upto = jnp.int32(0)
        total = 0

        def arrivals(index):
            first = 0 if index == 0 else UPTO[index - 1]
            for slot, part, way, _source in HOPS[first:UPTO[index]]:
                event(slot, part, way)

        for index in range(len(UNITS)):
            @pl.when(step == index)
            def _():
                arrivals(2 * index)
                for slot in READY[index]:
                    for part in range(4):
                        sib_arrival(slot, part).wait_recv()
                if index == 0:
                    for dy, dk in line:
                        eo_arrival(dy, dk).wait_recv()
                    for block in range(3):
                        value = jnp.zeros((8, 128), jnp.float32)
                        for r in range(8):
                            value = jnp.where(lane // SUB == r, eo_block[block * 8 + r], value)
                        eo_lane[block] = value

            total += len(READY[index])
            split_upto = jnp.where(step == index, jnp.int32(total), split_upto)

        def one_split(index, carry):
            split(index)
            return carry

        lax.fori_loop(split_done, split_upto, one_split, 0)

        left, right = pick(step, core, 0), pick(step, core, 1)
        weight = pick(step, core, 2)
        scale = jnp.where(weight == 2, jnp.float32(0.5), jnp.float32(1.0))

        dot = functools.partial(lax.dot_general, dimension_numbers=contract, preferred_element_type=jnp.float32)
        wide = dot(both[left, :ROWS], both[right])
        tile[...] = wide[:, :ROWS] + wide[:, ROWS:]

        for index in range(len(UNITS)):
            if UPTO[2 * index] < UPTO[2 * index + 1]:
                pl.when(step == index)(functools.partial(arrivals, 2 * index + 1))

        tile[...] += dot(both[left, ROWS:], both[right, :ROWS])

        down = evs[left, :16, :] * scale
        across = evs[right, 16:, :]
        for block_j in range(3):
            lanes = pl.ds(block_j * 128, 128)
            row = across - eo_lane[block_j]
            for block_i in range(block_j + 1):
                mirror = swap_pairs(
                    [tile[(block_j * 8 + r) * SUB:(block_j * 8 + r + 1) * SUB, block_i * 128:block_i * 128 + 128] for r in range(8)],
                    lax.broadcasted_iota(jnp.int32, (SUB, 128), 1),
                )
                for r in range(8):
                    i = block_i * 8 + r
                    here = tile[i * SUB:(i + 1) * SUB, lanes]
                    shift = (row - eo_block[i]) * scale
                    denom = down + jnp.concatenate([shift, shift], axis=0)
                    guess = pl.reciprocal(denom, approx=True)
                    inverse = guess * (2.0 - denom * guess)
                    term = (here * (here - mirror[r]) + mirror[r] * mirror[r]) * inverse
                    acc[i, :, lanes] = acc[i, :, lanes] + (term[:8] + term[8:])
        return split_upto

    lax.fori_loop(0, len(UNITS), step_body, jnp.int32(0))

    member = lax.broadcasted_iota(jnp.int32, (128, ROWS), 1) // SUB == lax.broadcasted_iota(jnp.int32, (128, ROWS), 0)
    group = member.astype(jnp.float32)
    summed = jnp.concatenate([jnp.sum(acc[...], axis=1), jnp.zeros((128 - OCC, ROWS), jnp.float32)], axis=0)
    exact = functools.partial(
        lax.dot_general, dimension_numbers=contract,
        precision=lax.Precision.HIGHEST, preferred_element_type=jnp.float32,
    )
    upper, lower = exact(summed, group), exact(group, summed)
    below = lax.broadcasted_iota(jnp.int32, (128, 128), 0) // 8 > lax.broadcasted_iota(jnp.int32, (128, 128), 1) // 8
    pairs = upper + jnp.where(below, lower, 0.0)

    rows_out[...] = jnp.zeros_like(rows_out)
    for owner in range(8):
        rows_out[owner, 0:3, :] = pairs[owner * 3:owner * 3 + 3, :]

    def red_copy(dy, dk):
        far = line_device(dy, dk)
        return pltpu.make_async_remote_copy(
            src_ref=rows_out.at[far[0]], dst_ref=rows_got.at[occ],
            send_sem=red_out.at[dy, dk], recv_sem=red_in.at[dy, dk],
            device_id=far, device_id_type=MESH,
        )

    def red_arrival(dy, dk):
        near = line_device((4 - dy) % 4, dk)
        return pltpu.make_async_remote_copy(
            src_ref=rows_out.at[occ], dst_ref=rows_got.at[near[0]],
            send_sem=red_out.at[dy, dk], recv_sem=red_in.at[dy, dk],
            device_id=near, device_id_type=MESH,
        )

    for dy, dk in line:
        red_copy(dy, dk).start()
    rows_got[occ] = rows_out[occ]
    for dy, dk in line:
        red_arrival(dy, dk).wait_recv()
    value = functools.reduce(lambda p, q: p + q, [rows_got[owner] for owner in range(8)])

    sent = []
    for axis, (place, got) in enumerate(((x, x_got), (z, z_got))):
        got[place] = value
        copies = []
        for d in range(1, 4):
            far = device((x + d) % 4, y, z, core) if axis == 0 else device(x, y, (z + d) % 4, core)
            copy = pltpu.make_async_remote_copy(
                src_ref=got.at[place], dst_ref=got.at[place],
                send_sem=plane_out.at[axis, d], recv_sem=plane_in.at[axis, d],
                device_id=far, device_id_type=MESH,
            )
            copy.start()
            sent.append(copy)
        for d in range(1, 4):
            source = (place + 4 - d) % 4
            pltpu.make_async_remote_copy(
                src_ref=got.at[place], dst_ref=got.at[source],
                send_sem=plane_out.at[axis, d], recv_sem=plane_in.at[axis, d],
                device_id=far, device_id_type=MESH,
            ).wait_recv()
        value = (got[0] + got[1]) + (got[2] + got[3])
    out_ref[...] = -value[:3, :OCC]

    for copy in sent:
        copy.wait_send()
    for dy, dk in line:
        red_copy(dy, dk).wait_send()
    for dy, dk in line:
        row_copy(dy, dk).wait_send()
        eo_copy(dy, dk).wait_send()
    for slot, part, way, source in HOPS:
        sib_copy(slot, part).wait_send()
        if way >= 0:
            hop_copy(slot, part, way, source).wait_send()
    for slot, (source, way) in EPS_FROM.items():
        ev_copy(slot, way, source).wait_send()


def on_device(factors, eps_occ, eps_vir):
    f32, dma = jnp.float32, pltpu.SemaphoreType.DMA
    return pl.pallas_call(
        kernel,
        out_shape=jax.ShapeDtypeStruct((3, OCC), f32),
        in_specs=[
            pl.BlockSpec(memory_space=pltpu.SMEM),
            pl.BlockSpec(memory_space=pltpu.SMEM),
            pl.BlockSpec(memory_space=pltpu.VMEM),
        ],
        out_specs=pl.BlockSpec(memory_space=pltpu.VMEM),
        scratch_shapes=[
            pltpu.VMEM((SLOTS, OCC, SUB, NAUX), f32),
            pltpu.VMEM((SLOTS, 2 * ROWS, NAUX), jnp.bfloat16),
            pltpu.VMEM((ROWS, ROWS), f32),
            pltpu.VMEM((OCC, 8, ROWS), f32),
            pltpu.VMEM((SLOTS, 24, 128), f32),
            pltpu.VMEM((OCC, 8, 128), f32),
            pltpu.VMEM((3, 8, 128), f32),
            pltpu.VMEM((8, 8, 128), f32), pltpu.VMEM((8, 8, 128), f32),
            pltpu.VMEM((4, 8, 128), f32), pltpu.VMEM((4, 8, 128), f32),
            dma((SLOTS, 4)), dma((SLOTS, 4)),
            dma((SLOTS, 4)), dma((SLOTS, 4)),
            dma((4, 2)), dma((4, 2)),
            dma((SLOTS,)), dma((SLOTS,)),
            dma((4, 2)), dma((4, 2)),
            dma,
            dma((4, 2)), dma((4, 2)), dma((2, 4)), dma((2, 4)),
        ],
        compiler_params=pltpu.CompilerParams(
            collective_id=0, has_side_effects=True, vmem_limit_bytes=61 * 2**20
        ),
        cost_estimate=pl.CostEstimate(flops=45 * 10**9, bytes_accessed=2 * 10**6, transcendentals=0),
    )(eps_occ, eps_vir, factors)


def solution(mesh):
    placed = (P("occ", ("va", "vb"), None), P("occ"), P(("va", "vb")))
    return jax.shard_map(on_device, mesh=mesh, in_specs=placed, out_specs=P("occ", None), check_vma=False)
```

```python
import functools

import jax
import jax.numpy as jnp
from jax import lax
from jax.experimental import pallas as pl
from jax.experimental.pallas import tpu as pltpu
from jax.sharding import PartitionSpec as P

MESH = pl.DeviceIdType.MESH
STEPS = ((1, 0, 0), (3, 0, 0), (0, 1, 0), (0, 3, 0), (0, 0, 1), (0, 0, 3))
OCC, SUB, NAUX = 24, 16, 1408
ROWS = OCC * SUB

POINTS = ((0, 0, 0), (0, 0, 3), (3, 0, 0), (1, 0, 0), (3, 0, 1), (0, 1, 0), (0, 3, 3), (2, 0, 0), (2, 0, 1), (0, 3, 2), (0, 2, 0), (0, 2, 2))
HOPS = (
    (0, 0, -1, -1),
    (0, 1, -1, -1),
    (0, 3, -1, -1),
    (1, 0, 5, 0),
    (3, 0, 0, 0),
    (2, 0, 1, 0),
    (0, 2, -1, -1),
    (1, 1, 5, 0),
    (3, 1, 0, 0),
    (2, 1, 1, 0),
    (4, 0, 4, 2),
    (5, 0, 2, 0),
    (6, 0, 3, 1),
    (1, 3, 5, 0),
    (3, 3, 0, 0),
    (2, 3, 1, 0),
    (4, 1, 4, 2),
    (5, 1, 2, 0),
    (6, 1, 3, 1),
    (1, 2, 5, 0),
    (7, 0, 0, 3),
    (2, 2, 1, 0),
    (4, 3, 4, 2),
    (5, 3, 2, 0),
    (6, 3, 3, 1),
    (9, 0, 5, 6),
    (3, 2, 0, 0),
    (7, 1, 1, 2),
    (4, 2, 4, 2),
    (5, 2, 2, 0),
    (6, 2, 3, 1),
    (9, 1, 5, 6),
    (7, 3, 0, 3),
    (8, 0, 1, 4),
    (8, 1, 4, 7),
    (10, 0, 2, 5),
    (11, 0, 3, 9),
    (9, 3, 5, 6),
    (7, 2, 0, 3),
    (8, 2, 1, 4),
    (8, 3, 4, 7),
    (10, 1, 2, 5),
    (11, 1, 3, 9),
    (9, 2, 5, 6),
    (10, 3, 2, 5),
    (11, 3, 3, 9),
    (10, 2, 2, 5),
    (11, 2, 3, 9),
)
UPTO = (
    22, 23, 23, 28, 29, 29, 31, 34, 34, 35, 37, 40,
    40, 41, 43, 44, 44, 44, 44, 46, 46, 46, 46, 46,
    48, 48, 48, 48, 48, 48, 48, 48, 48, 48, 48, 48,
)
UNITS = (
    ((0, 0, 1), (1, 0, 2)),
    ((2, 1, 2), (0, 2, 2)),
    ((3, 2, 1), (3, 1, 2)),
    ((3, 4, 2), (1, 4, 2)),
    ((2, 5, 2), (1, 5, 2)),
    ((3, 5, 2), (4, 5, 2)),
    ((5, 0, 2), (6, 5, 2)),
    ((2, 6, 2), (3, 6, 2)),
    ((4, 6, 2), (7, 5, 2)),
    ((6, 7, 2), (8, 5, 2)),
    ((1, 8, 1), (8, 6, 2)),
    ((4, 9, 2), (9, 5, 1)),
    ((9, 0, 2), (3, 9, 2)),
    ((4, 10, 2), (10, 6, 2)),
    ((3, 10, 2), (7, 10, 1)),
    ((10, 8, 2), (10, 0, 1)),
    ((11, 7, 1), (11, 3, 2)),
    ((11, 10, 1), (11, 4, 2)),
)

SLOTS = len(POINTS)
LAST = {slot: part for slot, part, _way, _from in HOPS}
CHILDREN = {}
for _slot, _part, _way, _from in HOPS:
    if _way >= 0:
        CHILDREN.setdefault((_from, _part), []).append((_slot, _way))
EPS_FROM = {slot: (source, way) for slot, part, way, source in HOPS if part == 0 and way >= 0}
READY = []
_seen = set()
for _pair in UNITS:
    _new = sorted({slot for unit in _pair for slot in unit[:2]} - _seen)
    _seen.update(_new)
    READY.append(_new)


PACK = 7


def words(core, field):
    out = []
    for start in range(0, len(UNITS), PACK):
        pair = [sum(u[side][field] << (4 * n) for n, u in enumerate(UNITS[start:start + PACK])) for side in range(2)]
        out.append(jnp.where(core == 0, jnp.int32(pair[0]), jnp.int32(pair[1])))
    return out


def pick(step, table):
    word = table[-1]
    for n in range(len(table) - 1, 0, -1):
        word = jnp.where(step < n * PACK, table[n - 1], word)
    return lax.shift_right_logical(word, 4 * lax.rem(step, PACK)) & 15


def swap_pairs(rows, lane):
    rows = list(rows)
    for bit in (4, 2, 1):
        low = (lane // (16 * bit)) % 2 == 0
        for r in range(8):
            if r & bit:
                continue
            first, second = rows[r], rows[r + bit]
            rows[r] = jnp.where(low, first, pltpu.roll(second, 16 * bit, 1))
            rows[r + bit] = jnp.where(low, pltpu.roll(first, 128 - 16 * bit, 1), second)
    return rows


def kernel(
    eps_occ, eps_vir, b_ref, out_ref,
    held, both, tile, done, acc, evs, eo_block, eo_lane,
    rows_out, rows_got, plane_got,
    hop_out, hop_in, sib_out, sib_in, row_out, row_in, ev_out, ev_in, eo_out, eo_in, own_sem,
    red_out, red_in, plane_out, plane_in,
):
    occ, va, vb = lax.axis_index("occ"), lax.axis_index("va"), lax.axis_index("vb")
    y, core = occ >> 1, occ & 1
    x, z = vb >> 1, (vb & 1) * 2 + va
    other = 1 - core

    def device(cx, cy, cz, ck):
        return (cy * 2 + ck, cz & 1, cx * 2 + (cz >> 1))

    xs, ys, zs = ([(place + d) & 3 for d in range(4)] for place in (x, y, z))
    sibling = device(x, y, z, other)
    near = [device(xs[(4 - dx) % 4], ys[(4 - dy) % 4], zs[(4 - dz) % 4], core) for dx, dy, dz in STEPS]
    quarter = [place * 6 for place in ys]
    half = (pl.multiple_of(core * 8, 8), pl.multiple_of(other * 8, 8))
    line = [(dy, dk) for dy in range(4) for dk in range(2) if (dy, dk) != (0, 0)]
    line_at = {(dy, dk): device(x, ys[dy], z, other if dk else core) for dy in range(4) for dk in range(2)}

    def to_step(way):
        return near[way]

    def line_device(dy, dk):
        return line_at[dy, dk]

    barrier = pltpu.get_barrier_semaphore()
    partners = [line_device(dy, dk) for dy, dk in line]
    partners += [device(xs[dx], y, zs[dz], core) for dx in range(4) for dz in range(4) if (dx, dz) != (0, 0)]
    for partner in partners:
        pl.semaphore_signal(barrier, inc=1, device_id=partner, device_id_type=MESH)
    pl.semaphore_wait(barrier, len(partners))

    def piece(slot, part, side):
        start = quarter[(POINTS[slot][1] + part) % 4]
        return held.at[slot, pl.ds(start, 6), pl.ds(half[side], 8), :]

    def row_copy(dy, dk):
        far = line_device(dy, dk)
        far_occ = far[0]
        return pltpu.make_async_remote_copy(
            src_ref=b_ref.at[:, pl.ds(pl.multiple_of(far_occ * 8, 8), 8), :],
            dst_ref=held.at[0, pl.ds(occ * 3, 3), pl.ds(half[dk], 8), :],
            send_sem=row_out.at[dy, dk], recv_sem=row_in.at[dy, dk],
            device_id=far, device_id_type=MESH,
        )

    def row_arrival(dy, dk):
        source = line_device((4 - dy) % 4, dk)
        place = held.at[0, pl.ds(source[0] * 3, 3), pl.ds(half[0], 8), :]
        return pltpu.make_async_remote_copy(
            src_ref=place, dst_ref=place, send_sem=row_out.at[dy, dk], recv_sem=row_in.at[dy, dk],
            device_id=source, device_id_type=MESH,
        )

    def sib_copy(slot, side):
        place = held.at[slot, :, pl.ds(half[side], 8), :]
        return pltpu.make_async_remote_copy(
            src_ref=place, dst_ref=place, send_sem=sib_out.at[slot], recv_sem=sib_in.at[slot],
            device_id=sibling, device_id_type=MESH,
        )

    def hop_copy(slot, part, way, source):
        return pltpu.make_async_remote_copy(
            src_ref=piece(source, part, 0),
            dst_ref=held.at[
                slot,
                pl.ds(quarter[(POINTS[source][1] + part) % 4], 6),
                pl.ds(half[0], 8),
                :,
            ],
            send_sem=hop_out.at[slot, part], recv_sem=hop_in.at[slot, part],
            device_id=to_step(way), device_id_type=MESH,
        )

    def hop_arrival(slot, part, way):
        return pltpu.make_async_remote_copy(
            src_ref=piece(slot, part, 0), dst_ref=piece(slot, part, 0),
            send_sem=hop_out.at[slot, part], recv_sem=hop_in.at[slot, part],
            device_id=to_step(way), device_id_type=MESH,
        )

    def ev_copy(slot, way, source):
        return pltpu.make_async_remote_copy(
            src_ref=evs.at[source], dst_ref=evs.at[slot], send_sem=ev_out.at[slot], recv_sem=ev_in.at[slot],
            device_id=to_step(way), device_id_type=MESH,
        )

    def eo_copy(dy, dk):
        return pltpu.make_async_remote_copy(
            src_ref=eo_block.at[pl.ds(occ * 3, 3)], dst_ref=eo_block.at[pl.ds(occ * 3, 3)],
            send_sem=eo_out.at[dy, dk], recv_sem=eo_in.at[dy, dk],
            device_id=line_device(dy, dk), device_id_type=MESH,
        )

    def eo_arrival(dy, dk):
        source = line_device((4 - dy) % 4, dk)
        place = eo_block.at[pl.ds(source[0] * 3, 3)]
        return pltpu.make_async_remote_copy(
            src_ref=place, dst_ref=place, send_sem=eo_out.at[dy, dk], recv_sem=eo_in.at[dy, dk],
            device_id=source, device_id_type=MESH,
        )

    own = pltpu.make_async_copy(
        b_ref.at[:, pl.ds(pl.multiple_of(occ * 8, 8), 8), :],
        held.at[0, pl.ds(occ * 3, 3), pl.ds(half[0], 8), :],
        own_sem,
    )
    row_copy(0, 1).start()
    own.start()
    for dy, dk in line[1:]:
        if dy != 2:
            row_copy(dy, dk).start()
    for dk in range(2):
        row_copy(2, dk).start()

    lane = lax.broadcasted_iota(jnp.int32, (8, 128), 1)
    sub16 = lax.broadcasted_iota(jnp.int32, (16, 128), 0)
    down = jnp.zeros((16, 128), jnp.float32)
    across = jnp.zeros((8, 128), jnp.float32)
    for a in range(SUB):
        value = eps_vir[y * SUB + a]
        down = jnp.where(sub16 == a, value, down)
        across = jnp.where(lane % SUB == a, value, across)
    evs[0, :16, :] = down
    evs[0, 16:, :] = across
    for r in range(3):
        eo_block[occ * 3 + r] = jnp.full((8, 128), eps_occ[r], jnp.float32)
    for slot, (source, way) in EPS_FROM.items():
        if source == 0:
            ev_copy(slot, way, source).start()
    for dy, dk in line:
        eo_copy(dy, dk).start()
    acc[...] = jnp.zeros_like(acc)
    done[...] = jnp.zeros_like(done)

    def event(slot, part, way):
        if slot == 0:
            dy = (4 - part) % 4
            for dk in range(2):
                if (dy, dk) == (0, 0):
                    own.wait()
                else:
                    row_arrival(dy, dk).wait_recv()
        else:
            hop_arrival(slot, part, way).wait_recv()
        for child, child_way in CHILDREN.get((slot, part), []):
            hop_copy(child, part, child_way, slot).start()
        if LAST[slot] == part:
            sib_copy(slot, 0).start()
        if part == 0 and slot:
            source, ev_way = EPS_FROM[slot]
            ev_copy(slot, ev_way, source).wait_recv()
            for child, (child_from, child_way) in EPS_FROM.items():
                if child_from == slot:
                    ev_copy(child, child_way, slot).start()

    def split(slot):
        def rows(i, carry):
            value = held[slot, i]
            top = value.astype(jnp.bfloat16)
            at = pl.ds(pl.multiple_of(i * SUB, SUB), SUB)
            both[slot, at, :] = top
            both[slot, pl.ds(pl.multiple_of(ROWS + i * SUB, SUB), SUB), :] = (value - top.astype(jnp.float32)).astype(jnp.bfloat16)
            return carry
        lax.fori_loop(0, OCC, rows, 0)

    contract = (((1,), (1,)), ((), ()))

    tables = [words(core, field) for field in range(3)]

    def energies(left, right, weight):
        scale = jnp.where(weight == 2, jnp.float32(0.5), jnp.float32(1.0))
        down = evs[left, :16, :] * scale
        across = evs[right, 16:, :]
        for block_j in range(3):
            lanes = pl.ds(block_j * 128, 128)
            row = across - eo_lane[block_j]
            for block_i in range(block_j + 1):
                mirror = swap_pairs(
                    [done[(block_j * 8 + r) * SUB:(block_j * 8 + r + 1) * SUB, block_i * 128:block_i * 128 + 128] for r in range(8)],
                    lax.broadcasted_iota(jnp.int32, (SUB, 128), 1),
                )
                for r in range(8):
                    i = block_i * 8 + r
                    here = done[i * SUB:(i + 1) * SUB, lanes]
                    shift = (row - eo_block[i]) * scale
                    denom = down + jnp.concatenate([shift, shift], axis=0)
                    guess = pl.reciprocal(denom, approx=True)
                    inverse = guess * (2.0 - denom * guess)
                    term = (here * (here - mirror[r]) + mirror[r] * mirror[r]) * inverse
                    acc[i, :, lanes] = acc[i, :, lanes] + (term[:8] + term[8:])

    def step_body(step, carry):
        split_done, old_left, old_right, old_weight = carry

        def arrivals(index):
            first = 0 if index == 0 else UPTO[index - 1]
            for slot, part, way, _source in HOPS[first:UPTO[index]]:
                event(slot, part, way)

        def before(index):
            arrivals(2 * index)
            for slot in READY[index]:
                sib_copy(slot, 1).wait_recv()
            if index == 0:
                for dy, dk in line:
                    eo_arrival(dy, dk).wait_recv()
                for block in range(3):
                    value = jnp.zeros((8, 128), jnp.float32)
                    for r in range(8):
                        value = jnp.where(lane // SUB == r, eo_block[block * 8 + r], value)
                    eo_lane[block] = value

        def between(index):
            arrivals(2 * index + 1)

        def choose(function, wanted):
            wanted = [index for index in range(len(UNITS)) if wanted(index)]
            for start in range(0, len(wanted), 4):
                some = wanted[start:start + 4]

                @pl.when((step >= some[0]) & (step <= some[-1]))
                def _():
                    for index in some:
                        pl.when(step == index)(functools.partial(function, index))

        choose(before, lambda index: READY[index] or UPTO[2 * index] > (UPTO[2 * index - 1] if index else 0))
        split_upto = jnp.int32(0)
        for index in range(len(UNITS)):
            if READY[index]:
                split_upto = split_upto + jnp.where(step >= index, jnp.int32(len(READY[index])), 0)

        def one_split(index, carry):
            split(index)
            return carry

        lax.fori_loop(split_done, split_upto, one_split, 0)

        left, right, weight = (pick(step, table) for table in tables)
        dot = functools.partial(lax.dot_general, dimension_numbers=contract, preferred_element_type=jnp.float32)
        wide = dot(both[left, :ROWS], both[right])
        tile[...] = wide[:, :ROWS] + wide[:, ROWS:]
        energies(old_left, old_right, old_weight)

        choose(between, lambda index: UPTO[2 * index] < UPTO[2 * index + 1])

        done[...] = tile[...] + dot(both[left, ROWS:], both[right, :ROWS])

        return split_upto, left, right, weight

    zero = jnp.int32(0)
    _, left, right, weight = lax.fori_loop(0, len(UNITS), step_body, (zero, zero, zero, zero))
    energies(left, right, weight)

    member = lax.broadcasted_iota(jnp.int32, (128, ROWS), 1) // SUB == lax.broadcasted_iota(jnp.int32, (128, ROWS), 0)
    group = member.astype(jnp.float32)
    summed = jnp.concatenate([jnp.sum(acc[...], axis=1), jnp.zeros((128 - OCC, ROWS), jnp.float32)], axis=0)
    exact = functools.partial(
        lax.dot_general, dimension_numbers=contract,
        precision=lax.Precision.HIGHEST, preferred_element_type=jnp.float32,
    )
    upper, lower = exact(summed, group), exact(group, summed)
    below = lax.broadcasted_iota(jnp.int32, (128, 128), 0) // 8 > lax.broadcasted_iota(jnp.int32, (128, 128), 1) // 8
    pairs = upper + jnp.where(below, lower, 0.0)

    rows_out[...] = jnp.zeros_like(rows_out)
    for owner in range(8):
        rows_out[owner, 0:3, :] = pairs[owner * 3:owner * 3 + 3, :]

    def red_copy(dy, dk):
        far = line_device(dy, dk)
        return pltpu.make_async_remote_copy(
            src_ref=rows_out.at[far[0]], dst_ref=rows_got.at[occ],
            send_sem=red_out.at[dy, dk], recv_sem=red_in.at[dy, dk],
            device_id=far, device_id_type=MESH,
        )

    def red_arrival(dy, dk):
        source = line_device((4 - dy) % 4, dk)
        return pltpu.make_async_remote_copy(
            src_ref=rows_out.at[occ], dst_ref=rows_got.at[source[0]],
            send_sem=red_out.at[dy, dk], recv_sem=red_in.at[dy, dk],
            device_id=source, device_id_type=MESH,
        )

    for dy, dk in line:
        red_copy(dy, dk).start()
    for slot in range(SLOTS):
        sib_copy(slot, 0).wait_send()
    for slot, part, way, source in HOPS:
        if way >= 0:
            hop_copy(slot, part, way, source).wait_send()
    rows_got[occ] = rows_out[occ]
    for dy, dk in line:
        red_arrival(dy, dk).wait_recv()
    value = functools.reduce(lambda p, q: p + q, [rows_got[owner] for owner in range(8)])

    place = x * 4 + z
    plane_got[place] = value
    plane = [(dx, dz) for dx in (2, 1, 3, 0) for dz in (2, 1, 3, 0) if (dx, dz) != (0, 0)]

    def plane_copy(dx, dz, to):
        far = device(xs[dx], y, zs[dz], core)
        return pltpu.make_async_remote_copy(
            src_ref=plane_got.at[place], dst_ref=plane_got.at[to],
            send_sem=plane_out.at[dx, dz], recv_sem=plane_in.at[dx, dz],
            device_id=far, device_id_type=MESH,
        )

    for dx, dz in plane:
        plane_copy(dx, dz, place).start()
    for slot, (source, way) in EPS_FROM.items():
        ev_copy(slot, way, source).wait_send()
    for dy, dk in line:
        row_copy(dy, dk).wait_send()
        eo_copy(dy, dk).wait_send()
        red_copy(dy, dk).wait_send()
    for dx, dz in plane:
        plane_copy(dx, dz, xs[(4 - dx) % 4] * 4 + zs[(4 - dz) % 4]).wait_recv()
    value = functools.reduce(lambda p, q: p + q, [plane_got[n] for n in range(16)])
    out_ref[...] = -value[:3, :OCC]
    for dx, dz in plane:
        plane_copy(dx, dz, place).wait_send()


def on_device(factors, eps_occ, eps_vir):
    f32, dma = jnp.float32, pltpu.SemaphoreType.DMA
    return pl.pallas_call(
        kernel,
        out_shape=jax.ShapeDtypeStruct((3, OCC), f32),
        in_specs=[
            pl.BlockSpec(memory_space=pltpu.SMEM),
            pl.BlockSpec(memory_space=pltpu.SMEM),
            pl.BlockSpec(memory_space=pltpu.VMEM),
        ],
        out_specs=pl.BlockSpec(memory_space=pltpu.VMEM),
        scratch_shapes=[
            pltpu.VMEM((SLOTS, OCC, SUB, NAUX), f32),
            pltpu.VMEM((SLOTS, 2 * ROWS, NAUX), jnp.bfloat16),
            pltpu.VMEM((ROWS, ROWS), f32), pltpu.VMEM((ROWS, ROWS), f32),
            pltpu.VMEM((OCC, 8, ROWS), f32),
            pltpu.VMEM((SLOTS, 24, 128), f32),
            pltpu.VMEM((OCC, 8, 128), f32),
            pltpu.VMEM((3, 8, 128), f32),
            pltpu.VMEM((8, 8, 128), f32), pltpu.VMEM((8, 8, 128), f32),
            pltpu.VMEM((16, 8, 128), f32),
            dma((SLOTS, 4)), dma((SLOTS, 4)),
            dma((SLOTS,)), dma((SLOTS,)),
            dma((4, 2)), dma((4, 2)),
            dma((SLOTS,)), dma((SLOTS,)),
            dma((4, 2)), dma((4, 2)),
            dma,
            dma((4, 2)), dma((4, 2)), dma((4, 4)), dma((4, 4)),
        ],
        compiler_params=pltpu.CompilerParams(
            collective_id=0, has_side_effects=True, vmem_limit_bytes=61 * 2**20
        ),
        cost_estimate=pl.CostEstimate(flops=45 * 10**9, bytes_accessed=2 * 10**6, transcendentals=0),
    )(eps_occ, eps_vir, factors)


def solution(mesh):
    placed = (P("occ", ("va", "vb"), None), P("occ"), P(("va", "vb")))
    return jax.shard_map(on_device, mesh=mesh, in_specs=placed, out_specs=P("occ", None), check_vma=False)
```

```python
import functools

import jax
import jax.numpy as jnp
from jax import lax
from jax.experimental import pallas as pl
from jax.experimental.pallas import tpu as pltpu
from jax.sharding import PartitionSpec as P

MESH = pl.DeviceIdType.MESH
STEPS = ((1, 0, 0), (3, 0, 0), (0, 1, 0), (0, 3, 0), (0, 0, 1), (0, 0, 3))
OCC, SUB, NAUX = 24, 16, 1408
ROWS = OCC * SUB

POINTS = ((0, 0, 0), (0, 0, 3), (3, 0, 0), (1, 0, 0), (3, 0, 1), (0, 1, 0), (0, 3, 3), (2, 0, 0), (2, 0, 1), (0, 3, 2), (0, 2, 0), (0, 2, 2))
HOPS = (
    (0, 0, -1, -1),
    (0, 1, -1, -1),
    (0, 3, -1, -1),
    (1, 0, 5, 0),
    (3, 0, 0, 0),
    (2, 0, 1, 0),
    (0, 2, -1, -1),
    (1, 1, 5, 0),
    (3, 1, 0, 0),
    (2, 1, 1, 0),
    (4, 0, 4, 2),
    (5, 0, 2, 0),
    (6, 0, 3, 1),
    (1, 3, 5, 0),
    (3, 3, 0, 0),
    (2, 3, 1, 0),
    (4, 1, 4, 2),
    (5, 1, 2, 0),
    (6, 1, 3, 1),
    (1, 2, 5, 0),
    (7, 0, 0, 3),
    (2, 2, 1, 0),
    (4, 3, 4, 2),
    (5, 3, 2, 0),
    (6, 3, 3, 1),
    (9, 0, 5, 6),
    (3, 2, 0, 0),
    (7, 1, 1, 2),
    (4, 2, 4, 2),
    (5, 2, 2, 0),
    (6, 2, 3, 1),
    (9, 1, 5, 6),
    (7, 3, 0, 3),
    (8, 0, 1, 4),
    (8, 1, 4, 7),
    (10, 0, 2, 5),
    (11, 0, 3, 9),
    (9, 3, 5, 6),
    (7, 2, 0, 3),
    (8, 2, 1, 4),
    (8, 3, 4, 7),
    (10, 1, 2, 5),
    (11, 1, 3, 9),
    (9, 2, 5, 6),
    (10, 3, 2, 5),
    (11, 3, 3, 9),
    (10, 2, 2, 5),
    (11, 2, 3, 9),
)
UPTO = (
    22, 23, 23, 28, 29, 29, 31, 34, 34, 35, 37, 40,
    40, 41, 43, 44, 44, 44, 44, 46, 46, 46, 46, 46,
    48, 48, 48, 48, 48, 48, 48, 48, 48, 48, 48, 48,
)
UNITS = (
    ((0, 0, 1), (1, 0, 2)),
    ((2, 1, 2), (0, 2, 2)),
    ((3, 2, 1), (3, 1, 2)),
    ((3, 4, 2), (1, 4, 2)),
    ((2, 5, 2), (1, 5, 2)),
    ((3, 5, 2), (4, 5, 2)),
    ((5, 0, 2), (6, 5, 2)),
    ((2, 6, 2), (3, 6, 2)),
    ((4, 6, 2), (7, 5, 2)),
    ((6, 7, 2), (8, 5, 2)),
    ((1, 8, 1), (8, 6, 2)),
    ((4, 9, 2), (9, 5, 1)),
    ((9, 0, 2), (3, 9, 2)),
    ((4, 10, 2), (10, 6, 2)),
    ((3, 10, 2), (7, 10, 1)),
    ((10, 8, 2), (10, 0, 1)),
    ((11, 7, 1), (11, 3, 2)),
    ((11, 10, 1), (11, 4, 2)),
)

SLOTS = len(POINTS)
CHILDREN = {}
for _slot, _part, _way, _from in HOPS:
    if _way >= 0:
        CHILDREN.setdefault((_from, _part), []).append((_slot, _way))
EPS_FROM = {slot: (source, way) for slot, part, way, source in HOPS if part == 0 and way >= 0}
READY = []
_seen = set()
for _pair in UNITS:
    _new = sorted({slot for unit in _pair for slot in unit[:2]} - _seen)
    _seen.update(_new)
    READY.append(_new)


PACK = 7


def words(core, field):
    out = []
    for start in range(0, len(UNITS), PACK):
        pair = [sum(u[side][field] << (4 * n) for n, u in enumerate(UNITS[start:start + PACK])) for side in range(2)]
        out.append(jnp.where(core == 0, jnp.int32(pair[0]), jnp.int32(pair[1])))
    return out


def pick(step, table):
    word = table[-1]
    for n in range(len(table) - 1, 0, -1):
        word = jnp.where(step < n * PACK, table[n - 1], word)
    return lax.shift_right_logical(word, 4 * lax.rem(step, PACK)) & 15


def swap_pairs(rows, lane):
    rows = list(rows)
    for bit in (4, 2, 1):
        low = (lane // (16 * bit)) % 2 == 0
        for r in range(8):
            if r & bit:
                continue
            first, second = rows[r], rows[r + bit]
            rows[r] = jnp.where(low, first, pltpu.roll(second, 16 * bit, 1))
            rows[r + bit] = jnp.where(low, pltpu.roll(first, 128 - 16 * bit, 1), second)
    return rows


def kernel(
    eps_occ, eps_vir, b_ref, out_ref,
    held, both, done, acc, evs, eo_block, eo_lane,
    rows_out, rows_got, plane_got,
    hop_out, hop_in, sib_out, sib_in, row_out, row_in, ev_out, ev_in, eo_out, eo_in, own_sem,
    red_out, red_in, plane_out, plane_in,
):
    occ, va, vb = lax.axis_index("occ"), lax.axis_index("va"), lax.axis_index("vb")
    y, core = occ >> 1, occ & 1
    x, z = vb >> 1, (vb & 1) * 2 + va
    other = 1 - core

    def device(cx, cy, cz, ck):
        return (cy * 2 + ck, cz & 1, cx * 2 + (cz >> 1))

    xs, ys, zs = ([(place + d) & 3 for d in range(4)] for place in (x, y, z))
    sibling = device(x, y, z, other)
    near = [device(xs[(4 - dx) % 4], ys[(4 - dy) % 4], zs[(4 - dz) % 4], core) for dx, dy, dz in STEPS]
    quarter = [place * 6 for place in ys]
    half = (pl.multiple_of(core * 8, 8), pl.multiple_of(other * 8, 8))
    line = [(dy, dk) for dy in range(4) for dk in range(2) if (dy, dk) != (0, 0)]
    line_at = {(dy, dk): device(x, ys[dy], z, other if dk else core) for dy in range(4) for dk in range(2)}

    def to_step(way):
        return near[way]

    def line_device(dy, dk):
        return line_at[dy, dk]

    barrier = pltpu.get_barrier_semaphore()
    partners = [line_device(dy, dk) for dy, dk in line]
    partners += [device(xs[dx], y, zs[dz], core) for dx in range(4) for dz in range(4) if (dx, dz) != (0, 0)]
    for partner in partners:
        pl.semaphore_signal(barrier, inc=1, device_id=partner, device_id_type=MESH)
    pl.semaphore_wait(barrier, len(partners))

    def piece(slot, part, side):
        start = quarter[(POINTS[slot][1] + part) % 4]
        return held.at[slot, pl.ds(start, 6), pl.ds(half[side], 8), :]

    def row_copy(dy, dk):
        far = line_device(dy, dk)
        far_occ = far[0]
        return pltpu.make_async_remote_copy(
            src_ref=b_ref.at[:, pl.ds(pl.multiple_of(far_occ * 8, 8), 8), :],
            dst_ref=held.at[0, pl.ds(occ * 3, 3), pl.ds(half[dk], 8), :],
            send_sem=row_out.at[dy, dk], recv_sem=row_in.at[dy, dk],
            device_id=far, device_id_type=MESH,
        )

    def row_arrival(dy, dk):
        source = line_device((4 - dy) % 4, dk)
        place = held.at[0, pl.ds(source[0] * 3, 3), pl.ds(half[0], 8), :]
        return pltpu.make_async_remote_copy(
            src_ref=place, dst_ref=place, send_sem=row_out.at[dy, dk], recv_sem=row_in.at[dy, dk],
            device_id=source, device_id_type=MESH,
        )

    def sib_copy(slot, part, side):
        return pltpu.make_async_remote_copy(
            src_ref=piece(slot, part, side), dst_ref=piece(slot, part, side),
            send_sem=sib_out.at[slot, part], recv_sem=sib_in.at[slot, part],
            device_id=sibling, device_id_type=MESH,
        )

    def hop_copy(slot, part, way, source):
        return pltpu.make_async_remote_copy(
            src_ref=piece(source, part, 0),
            dst_ref=held.at[
                slot,
                pl.ds(quarter[(POINTS[source][1] + part) % 4], 6),
                pl.ds(half[0], 8),
                :,
            ],
            send_sem=hop_out.at[slot, part], recv_sem=hop_in.at[slot, part],
            device_id=to_step(way), device_id_type=MESH,
        )

    def hop_arrival(slot, part, way):
        return pltpu.make_async_remote_copy(
            src_ref=piece(slot, part, 0), dst_ref=piece(slot, part, 0),
            send_sem=hop_out.at[slot, part], recv_sem=hop_in.at[slot, part],
            device_id=to_step(way), device_id_type=MESH,
        )

    def ev_copy(slot, way, source):
        return pltpu.make_async_remote_copy(
            src_ref=evs.at[source], dst_ref=evs.at[slot], send_sem=ev_out.at[slot], recv_sem=ev_in.at[slot],
            device_id=to_step(way), device_id_type=MESH,
        )

    def eo_copy(dy, dk):
        return pltpu.make_async_remote_copy(
            src_ref=eo_block.at[pl.ds(occ * 3, 3)], dst_ref=eo_block.at[pl.ds(occ * 3, 3)],
            send_sem=eo_out.at[dy, dk], recv_sem=eo_in.at[dy, dk],
            device_id=line_device(dy, dk), device_id_type=MESH,
        )

    def eo_arrival(dy, dk):
        source = line_device((4 - dy) % 4, dk)
        place = eo_block.at[pl.ds(source[0] * 3, 3)]
        return pltpu.make_async_remote_copy(
            src_ref=place, dst_ref=place, send_sem=eo_out.at[dy, dk], recv_sem=eo_in.at[dy, dk],
            device_id=source, device_id_type=MESH,
        )

    own = pltpu.make_async_copy(
        b_ref.at[:, pl.ds(pl.multiple_of(occ * 8, 8), 8), :],
        held.at[0, pl.ds(occ * 3, 3), pl.ds(half[0], 8), :],
        own_sem,
    )
    row_copy(0, 1).start()
    own.start()
    for dy, dk in line[1:]:
        if dy != 2:
            row_copy(dy, dk).start()
    for dk in range(2):
        row_copy(2, dk).start()

    lane = lax.broadcasted_iota(jnp.int32, (8, 128), 1)
    sub16 = lax.broadcasted_iota(jnp.int32, (16, 128), 0)
    down = jnp.zeros((16, 128), jnp.float32)
    across = jnp.zeros((8, 128), jnp.float32)
    for a in range(SUB):
        value = eps_vir[y * SUB + a]
        down = jnp.where(sub16 == a, value, down)
        across = jnp.where(lane % SUB == a, value, across)
    evs[0, :16, :] = down
    evs[0, 16:, :] = across
    for r in range(3):
        eo_block[occ * 3 + r] = jnp.full((8, 128), eps_occ[r], jnp.float32)
    for slot, (source, way) in EPS_FROM.items():
        if source == 0:
            ev_copy(slot, way, source).start()
    for dy, dk in line:
        eo_copy(dy, dk).start()
    acc[...] = jnp.zeros_like(acc)
    done[...] = jnp.zeros_like(done)

    def event(slot, part, way):
        if slot == 0:
            dy = (4 - part) % 4
            for dk in range(2):
                if (dy, dk) == (0, 0):
                    own.wait()
                else:
                    row_arrival(dy, dk).wait_recv()
        else:
            hop_arrival(slot, part, way).wait_recv()
        for child, child_way in CHILDREN.get((slot, part), []):
            hop_copy(child, part, child_way, slot).start()
        sib_copy(slot, part, 0).start()
        if part == 0 and slot:
            source, ev_way = EPS_FROM[slot]
            ev_copy(slot, ev_way, source).wait_recv()
            for child, (child_from, child_way) in EPS_FROM.items():
                if child_from == slot:
                    ev_copy(child, child_way, slot).start()

    def split(slot):
        def rows(i, carry):
            value = held[slot, i]
            top = value.astype(jnp.bfloat16)
            at = pl.ds(pl.multiple_of(i * SUB, SUB), SUB)
            both[slot, at, :] = top
            both[slot, pl.ds(pl.multiple_of(ROWS + i * SUB, SUB), SUB), :] = (value - top.astype(jnp.float32)).astype(jnp.bfloat16)
            return carry
        lax.fori_loop(0, OCC, rows, 0)

    contract = (((1,), (1,)), ((), ()))

    tables = [words(core, field) for field in range(3)]

    def energies(left, right, weight):
        scale = jnp.where(weight == 2, jnp.float32(0.5), jnp.float32(1.0))
        down = evs[left, :16, :] * scale
        across = evs[right, 16:, :]
        for block_j in range(3):
            lanes = pl.ds(block_j * 128, 128)
            row = across - eo_lane[block_j]
            for block_i in range(block_j + 1):
                mirror = swap_pairs(
                    [done[(block_j * 8 + r) * SUB:(block_j * 8 + r + 1) * SUB, block_i * 128:block_i * 128 + 128] for r in range(8)],
                    lax.broadcasted_iota(jnp.int32, (SUB, 128), 1),
                )
                for r in range(8):
                    i = block_i * 8 + r
                    here = done[i * SUB:(i + 1) * SUB, lanes]
                    shift = (row - eo_block[i]) * scale
                    denom = down + jnp.concatenate([shift, shift], axis=0)
                    guess = pl.reciprocal(denom, approx=True)
                    inverse = guess * (2.0 - denom * guess)
                    term = (here * (here - mirror[r]) + mirror[r] * mirror[r]) * inverse
                    acc[i, :, lanes] = acc[i, :, lanes] + (term[:8] + term[8:])

    def step_body(step, carry):
        split_done, old_left, old_right, old_weight = carry

        def arrivals(index):
            first = 0 if index == 0 else UPTO[index - 2]
            for slot, part, way, _source in HOPS[first:UPTO[index]]:
                event(slot, part, way)

        def before(index):
            arrivals(2 * index)
            for slot in READY[index]:
                for part in range(4):
                    sib_copy(slot, part, 1).wait_recv()
            if index == 0:
                for dy, dk in line:
                    eo_arrival(dy, dk).wait_recv()
                for block in range(3):
                    value = jnp.zeros((8, 128), jnp.float32)
                    for r in range(8):
                        value = jnp.where(lane // SUB == r, eo_block[block * 8 + r], value)
                    eo_lane[block] = value

        def choose(function, wanted):
            wanted = [index for index in range(len(UNITS)) if wanted(index)]
            for start in range(0, len(wanted), 4):
                some = wanted[start:start + 4]

                @pl.when((step >= some[0]) & (step <= some[-1]))
                def _():
                    for index in some:
                        pl.when(step == index)(functools.partial(function, index))

        choose(before, lambda index: READY[index] or UPTO[2 * index] > (UPTO[2 * index - 2] if index else 0))
        split_upto = jnp.int32(0)
        for index in range(len(UNITS)):
            if READY[index]:
                split_upto = split_upto + jnp.where(step >= index, jnp.int32(len(READY[index])), 0)

        def one_split(index, carry):
            split(index)
            return carry

        lax.fori_loop(split_done, split_upto, one_split, 0)

        left, right, weight = (pick(step, table) for table in tables)
        dot = functools.partial(lax.dot_general, dimension_numbers=contract, preferred_element_type=jnp.float32)
        wide = dot(both[left, :ROWS], both[right])
        narrow = dot(both[left, ROWS:], both[right, :ROWS])
        energies(old_left, old_right, old_weight)
        done[...] = wide[:, :ROWS] + wide[:, ROWS:] + narrow
        return split_upto, left, right, weight

    zero = jnp.int32(0)
    _, left, right, weight = lax.fori_loop(0, len(UNITS), step_body, (zero, zero, zero, zero))
    energies(left, right, weight)

    member = lax.broadcasted_iota(jnp.int32, (128, ROWS), 1) // SUB == lax.broadcasted_iota(jnp.int32, (128, ROWS), 0)
    group = member.astype(jnp.float32)
    summed = jnp.concatenate([jnp.sum(acc[...], axis=1), jnp.zeros((128 - OCC, ROWS), jnp.float32)], axis=0)
    exact = functools.partial(
        lax.dot_general, dimension_numbers=contract,
        precision=lax.Precision.HIGHEST, preferred_element_type=jnp.float32,
    )
    upper, lower = exact(summed, group), exact(group, summed)
    below = lax.broadcasted_iota(jnp.int32, (128, 128), 0) // 8 > lax.broadcasted_iota(jnp.int32, (128, 128), 1) // 8
    pairs = upper + jnp.where(below, lower, 0.0)

    rows_out[...] = jnp.zeros_like(rows_out)
    for owner in range(8):
        rows_out[owner, 0:3, :] = pairs[owner * 3:owner * 3 + 3, :]

    def red_copy(dy, dk):
        far = line_device(dy, dk)
        return pltpu.make_async_remote_copy(
            src_ref=rows_out.at[far[0]], dst_ref=rows_got.at[occ],
            send_sem=red_out.at[dy, dk], recv_sem=red_in.at[dy, dk],
            device_id=far, device_id_type=MESH,
        )

    def red_arrival(dy, dk):
        source = line_device((4 - dy) % 4, dk)
        return pltpu.make_async_remote_copy(
            src_ref=rows_out.at[occ], dst_ref=rows_got.at[source[0]],
            send_sem=red_out.at[dy, dk], recv_sem=red_in.at[dy, dk],
            device_id=source, device_id_type=MESH,
        )

    for dy, dk in line:
        red_copy(dy, dk).start()
    for slot, part, way, source in HOPS:
        sib_copy(slot, part, 0).wait_send()
        if way >= 0:
            hop_copy(slot, part, way, source).wait_send()
    rows_got[occ] = rows_out[occ]
    for dy, dk in line:
        red_arrival(dy, dk).wait_recv()
    value = functools.reduce(lambda p, q: p + q, [rows_got[owner] for owner in range(8)])

    place = x * 4 + z
    plane_got[place] = value
    plane = [(dx, dz) for dx in (2, 1, 3, 0) for dz in (2, 1, 3, 0) if (dx, dz) != (0, 0)]

    def plane_copy(dx, dz, to):
        far = device(xs[dx], y, zs[dz], core)
        return pltpu.make_async_remote_copy(
            src_ref=plane_got.at[place], dst_ref=plane_got.at[to],
            send_sem=plane_out.at[dx, dz], recv_sem=plane_in.at[dx, dz],
            device_id=far, device_id_type=MESH,
        )

    for dx, dz in plane:
        plane_copy(dx, dz, place).start()
    for slot, (source, way) in EPS_FROM.items():
        ev_copy(slot, way, source).wait_send()
    for dy, dk in line:
        row_copy(dy, dk).wait_send()
        eo_copy(dy, dk).wait_send()
        red_copy(dy, dk).wait_send()
    for dx, dz in plane:
        plane_copy(dx, dz, xs[(4 - dx) % 4] * 4 + zs[(4 - dz) % 4]).wait_recv()
    value = functools.reduce(lambda p, q: p + q, [plane_got[n] for n in range(16)])
    out_ref[...] = -value[:3, :OCC]
    for dx, dz in plane:
        plane_copy(dx, dz, place).wait_send()


def on_device(factors, eps_occ, eps_vir):
    f32, dma = jnp.float32, pltpu.SemaphoreType.DMA
    return pl.pallas_call(
        kernel,
        out_shape=jax.ShapeDtypeStruct((3, OCC), f32),
        in_specs=[
            pl.BlockSpec(memory_space=pltpu.SMEM),
            pl.BlockSpec(memory_space=pltpu.SMEM),
            pl.BlockSpec(memory_space=pltpu.VMEM),
        ],
        out_specs=pl.BlockSpec(memory_space=pltpu.VMEM),
        scratch_shapes=[
            pltpu.VMEM((SLOTS, OCC, SUB, NAUX), f32),
            pltpu.VMEM((SLOTS, 2 * ROWS, NAUX), jnp.bfloat16),
            pltpu.VMEM((ROWS, ROWS), f32),
            pltpu.VMEM((OCC, 8, ROWS), f32),
            pltpu.VMEM((SLOTS, 24, 128), f32),
            pltpu.VMEM((OCC, 8, 128), f32),
            pltpu.VMEM((3, 8, 128), f32),
            pltpu.VMEM((8, 8, 128), f32), pltpu.VMEM((8, 8, 128), f32),
            pltpu.VMEM((16, 8, 128), f32),
            dma((SLOTS, 4)), dma((SLOTS, 4)),
            dma((SLOTS, 4)), dma((SLOTS, 4)),
            dma((4, 2)), dma((4, 2)),
            dma((SLOTS,)), dma((SLOTS,)),
            dma((4, 2)), dma((4, 2)),
            dma,
            dma((4, 2)), dma((4, 2)), dma((4, 4)), dma((4, 4)),
        ],
        compiler_params=pltpu.CompilerParams(
            collective_id=0, has_side_effects=True, vmem_limit_bytes=61 * 2**20
        ),
        cost_estimate=pl.CostEstimate(flops=45 * 10**9, bytes_accessed=2 * 10**6, transcendentals=0),
    )(eps_occ, eps_vir, factors)


def solution(mesh):
    placed = (P("occ", ("va", "vb"), None), P("occ"), P(("va", "vb")))
    return jax.shard_map(on_device, mesh=mesh, in_specs=placed, out_specs=P("occ", None), check_vma=False)
```

```python
import functools

import jax
import jax.numpy as jnp
from jax import lax
from jax.experimental import pallas as pl
from jax.experimental.pallas import tpu as pltpu
from jax.sharding import PartitionSpec as P

MESH = pl.DeviceIdType.MESH
STEPS = ((1, 0, 0), (3, 0, 0), (0, 1, 0), (0, 3, 0), (0, 0, 1), (0, 0, 3))
OCC, SUB, NAUX = 24, 16, 1408
ROWS = OCC * SUB

POINTS = ((0, 0, 0), (0, 0, 3), (3, 0, 0), (1, 0, 0), (3, 0, 1), (0, 1, 0), (0, 3, 3), (2, 0, 0), (2, 0, 1), (0, 3, 2), (0, 2, 0), (0, 2, 2))
HOPS = (
    (0, 0, -1, -1),
    (0, 1, -1, -1),
    (0, 3, -1, -1),
    (1, 0, 5, 0),
    (3, 0, 0, 0),
    (2, 0, 1, 0),
    (0, 2, -1, -1),
    (1, 1, 5, 0),
    (3, 1, 0, 0),
    (2, 1, 1, 0),
    (4, 0, 4, 2),
    (5, 0, 2, 0),
    (6, 0, 3, 1),
    (1, 3, 5, 0),
    (3, 3, 0, 0),
    (2, 3, 1, 0),
    (4, 1, 4, 2),
    (5, 1, 2, 0),
    (6, 1, 3, 1),
    (1, 2, 5, 0),
    (7, 0, 0, 3),
    (2, 2, 1, 0),
    (4, 3, 4, 2),
    (5, 3, 2, 0),
    (6, 3, 3, 1),
    (9, 0, 5, 6),
    (3, 2, 0, 0),
    (7, 1, 1, 2),
    (4, 2, 4, 2),
    (5, 2, 2, 0),
    (6, 2, 3, 1),
    (9, 1, 5, 6),
    (7, 3, 0, 3),
    (8, 0, 1, 4),
    (8, 1, 4, 7),
    (10, 0, 2, 5),
    (11, 0, 3, 9),
    (9, 3, 5, 6),
    (7, 2, 0, 3),
    (8, 2, 1, 4),
    (8, 3, 4, 7),
    (10, 1, 2, 5),
    (11, 1, 3, 9),
    (9, 2, 5, 6),
    (10, 3, 2, 5),
    (11, 3, 3, 9),
    (10, 2, 2, 5),
    (11, 2, 3, 9),
)
UPTO = (
    22, 23, 23, 28, 29, 29, 31, 34, 34, 35, 37, 40,
    40, 41, 43, 44, 44, 44, 44, 46, 46, 46, 46, 46,
    48, 48, 48, 48, 48, 48, 48, 48, 48, 48, 48, 48,
)
UNITS = (
    ((0, 0, 1), (1, 0, 2)),
    ((2, 1, 2), (0, 2, 2)),
    ((3, 2, 1), (3, 1, 2)),
    ((3, 4, 2), (1, 4, 2)),
    ((2, 5, 2), (1, 5, 2)),
    ((3, 5, 2), (4, 5, 2)),
    ((5, 0, 2), (6, 5, 2)),
    ((2, 6, 2), (3, 6, 2)),
    ((4, 6, 2), (7, 5, 2)),
    ((6, 7, 2), (8, 5, 2)),
    ((1, 8, 1), (8, 6, 2)),
    ((4, 9, 2), (9, 5, 1)),
    ((9, 0, 2), (3, 9, 2)),
    ((4, 10, 2), (10, 6, 2)),
    ((3, 10, 2), (7, 10, 1)),
    ((10, 8, 2), (10, 0, 1)),
    ((11, 7, 1), (11, 3, 2)),
    ((11, 10, 1), (11, 4, 2)),
)

SLOTS = len(POINTS)
CHILDREN = {}
for _slot, _part, _way, _from in HOPS:
    if _way >= 0:
        CHILDREN.setdefault((_from, _part), []).append((_slot, _way))
EPS_FROM = {slot: (source, way) for slot, part, way, source in HOPS if part == 0 and way >= 0}
READY = []
_seen = set()
for _pair in UNITS:
    _new = sorted({slot for unit in _pair for slot in unit[:2]} - _seen)
    _seen.update(_new)
    READY.append(_new)


PACK = 7


def words(core, field):
    out = []
    for start in range(0, len(UNITS), PACK):
        pair = [sum(u[side][field] << (4 * n) for n, u in enumerate(UNITS[start:start + PACK])) for side in range(2)]
        out.append(jnp.where(core == 0, jnp.int32(pair[0]), jnp.int32(pair[1])))
    return out


def pick(step, table):
    word = table[-1]
    for n in range(len(table) - 1, 0, -1):
        word = jnp.where(step < n * PACK, table[n - 1], word)
    return lax.shift_right_logical(word, 4 * lax.rem(step, PACK)) & 15


def swap_pairs(rows, lane):
    rows = list(rows)
    for bit in (4, 2, 1):
        low = (lane // (16 * bit)) % 2 == 0
        for r in range(8):
            if r & bit:
                continue
            first, second = rows[r], rows[r + bit]
            rows[r] = jnp.where(low, first, pltpu.roll(second, 16 * bit, 1))
            rows[r + bit] = jnp.where(low, pltpu.roll(first, 128 - 16 * bit, 1), second)
    return rows


def kernel(
    eps_occ, eps_vir, b_ref, out_ref,
    held, both, done, acc, evs, eo_block, eo_lane,
    rows_out, rows_got, plane_got,
    hop_out, hop_in, sib_out, sib_in, row_out, row_in, ev_out, ev_in, eo_out, eo_in, own_sem,
    red_out, red_in, plane_out, plane_in,
):
    occ, va, vb = lax.axis_index("occ"), lax.axis_index("va"), lax.axis_index("vb")
    y, core = occ >> 1, occ & 1
    x, z = vb >> 1, (vb & 1) * 2 + va
    other = 1 - core

    def device(cx, cy, cz, ck):
        return (cy * 2 + ck, cz & 1, cx * 2 + (cz >> 1))

    xs, ys, zs = ([(place + d) & 3 for d in range(4)] for place in (x, y, z))
    sibling = device(x, y, z, other)
    near = [device(xs[(4 - dx) % 4], ys[(4 - dy) % 4], zs[(4 - dz) % 4], core) for dx, dy, dz in STEPS]
    quarter = [place * 6 for place in ys]
    half = (pl.multiple_of(core * 8, 8), pl.multiple_of(other * 8, 8))
    line = [(dy, dk) for dy in range(4) for dk in range(2) if (dy, dk) != (0, 0)]
    line_at = {(dy, dk): device(x, ys[dy], z, other if dk else core) for dy in range(4) for dk in range(2)}

    def to_step(way):
        return near[way]

    def line_device(dy, dk):
        return line_at[dy, dk]

    barrier = pltpu.get_barrier_semaphore()
    partners = [line_device(dy, dk) for dy, dk in line]
    partners += [device(xs[dx], y, zs[dz], core) for dx in range(4) for dz in range(4) if (dx, dz) != (0, 0)]
    for partner in partners:
        pl.semaphore_signal(barrier, inc=1, device_id=partner, device_id_type=MESH)
    pl.semaphore_wait(barrier, len(partners))

    def piece(slot, part, side):
        start = quarter[(POINTS[slot][1] + part) % 4]
        return held.at[slot, pl.ds(start, 6), pl.ds(half[side], 8), :]

    def row_copy(dy, dk):
        far = line_device(dy, dk)
        far_occ = far[0]
        return pltpu.make_async_remote_copy(
            src_ref=b_ref.at[:, pl.ds(pl.multiple_of(far_occ * 8, 8), 8), :],
            dst_ref=held.at[0, pl.ds(occ * 3, 3), pl.ds(half[dk], 8), :],
            send_sem=row_out.at[dy, dk], recv_sem=row_in.at[dy, dk],
            device_id=far, device_id_type=MESH,
        )

    def row_arrival(dy, dk):
        source = line_device((4 - dy) % 4, dk)
        place = held.at[0, pl.ds(source[0] * 3, 3), pl.ds(half[0], 8), :]
        return pltpu.make_async_remote_copy(
            src_ref=place, dst_ref=place, send_sem=row_out.at[dy, dk], recv_sem=row_in.at[dy, dk],
            device_id=source, device_id_type=MESH,
        )

    def sib_copy(slot, part, side):
        return pltpu.make_async_remote_copy(
            src_ref=piece(slot, part, side), dst_ref=piece(slot, part, side),
            send_sem=sib_out.at[slot, part], recv_sem=sib_in.at[slot, part],
            device_id=sibling, device_id_type=MESH,
        )

    def hop_copy(slot, part, way, source):
        return pltpu.make_async_remote_copy(
            src_ref=piece(source, part, 0),
            dst_ref=held.at[
                slot,
                pl.ds(quarter[(POINTS[source][1] + part) % 4], 6),
                pl.ds(half[0], 8),
                :,
            ],
            send_sem=hop_out.at[slot, part], recv_sem=hop_in.at[slot, part],
            device_id=to_step(way), device_id_type=MESH,
        )

    def hop_arrival(slot, part, way):
        return pltpu.make_async_remote_copy(
            src_ref=piece(slot, part, 0), dst_ref=piece(slot, part, 0),
            send_sem=hop_out.at[slot, part], recv_sem=hop_in.at[slot, part],
            device_id=to_step(way), device_id_type=MESH,
        )

    def ev_copy(slot, way, source):
        return pltpu.make_async_remote_copy(
            src_ref=evs.at[source], dst_ref=evs.at[slot], send_sem=ev_out.at[slot], recv_sem=ev_in.at[slot],
            device_id=to_step(way), device_id_type=MESH,
        )

    def eo_copy(dy, dk):
        return pltpu.make_async_remote_copy(
            src_ref=eo_block.at[pl.ds(occ * 3, 3)], dst_ref=eo_block.at[pl.ds(occ * 3, 3)],
            send_sem=eo_out.at[dy, dk], recv_sem=eo_in.at[dy, dk],
            device_id=line_device(dy, dk), device_id_type=MESH,
        )

    def eo_arrival(dy, dk):
        source = line_device((4 - dy) % 4, dk)
        place = eo_block.at[pl.ds(source[0] * 3, 3)]
        return pltpu.make_async_remote_copy(
            src_ref=place, dst_ref=place, send_sem=eo_out.at[dy, dk], recv_sem=eo_in.at[dy, dk],
            device_id=source, device_id_type=MESH,
        )

    own = pltpu.make_async_copy(
        b_ref.at[:, pl.ds(pl.multiple_of(occ * 8, 8), 8), :],
        held.at[0, pl.ds(occ * 3, 3), pl.ds(half[0], 8), :],
        own_sem,
    )
    row_copy(0, 1).start()
    own.start()
    for dy, dk in line[1:]:
        if dy != 2:
            row_copy(dy, dk).start()
    for dk in range(2):
        row_copy(2, dk).start()

    lane = lax.broadcasted_iota(jnp.int32, (8, 128), 1)
    sub16 = lax.broadcasted_iota(jnp.int32, (16, 128), 0)
    down = jnp.zeros((16, 128), jnp.float32)
    across = jnp.zeros((8, 128), jnp.float32)
    for a in range(SUB):
        value = eps_vir[y * SUB + a]
        down = jnp.where(sub16 == a, value, down)
        across = jnp.where(lane % SUB == a, value, across)
    evs[0, :16, :] = down
    evs[0, 16:, :] = across
    for r in range(3):
        eo_block[occ * 3 + r] = jnp.full((8, 128), eps_occ[r], jnp.float32)
    for slot, (source, way) in EPS_FROM.items():
        if source == 0:
            ev_copy(slot, way, source).start()
    for dy, dk in line:
        eo_copy(dy, dk).start()
    acc[...] = jnp.zeros_like(acc)
    done[...] = jnp.zeros_like(done)

    def event(slot, part, way):
        if slot == 0:
            dy = (4 - part) % 4
            for dk in range(2):
                if (dy, dk) == (0, 0):
                    own.wait()
                else:
                    row_arrival(dy, dk).wait_recv()
        else:
            hop_arrival(slot, part, way).wait_recv()
        for child, child_way in CHILDREN.get((slot, part), []):
            hop_copy(child, part, child_way, slot).start()
        sib_copy(slot, part, 0).start()
        if part == 0 and slot:
            source, ev_way = EPS_FROM[slot]
            ev_copy(slot, ev_way, source).wait_recv()
            for child, (child_from, child_way) in EPS_FROM.items():
                if child_from == slot:
                    ev_copy(child, child_way, slot).start()

    def split(slot):
        def rows(i, carry):
            value = held[slot, i]
            top = value.astype(jnp.bfloat16)
            at = pl.ds(pl.multiple_of(i * SUB, SUB), SUB)
            both[slot, at, :] = top
            both[slot, pl.ds(pl.multiple_of(ROWS + i * SUB, SUB), SUB), :] = (value - top.astype(jnp.float32)).astype(jnp.bfloat16)
            return carry
        lax.fori_loop(0, OCC, rows, 0)

    contract = (((1,), (1,)), ((), ()))

    tables = [words(core, field) for field in range(3)]

    def energies(left, right, weight):
        scale = jnp.where(weight == 2, jnp.float32(0.5), jnp.float32(1.0))
        down = evs[left, :16, :] * scale
        across = evs[right, 16:, :]
        for block_j in range(3):
            lanes = pl.ds(block_j * 128, 128)
            row = across - eo_lane[block_j]
            for block_i in range(block_j + 1):
                mirror = swap_pairs(
                    [done[(block_j * 8 + r) * SUB:(block_j * 8 + r + 1) * SUB, block_i * 128:block_i * 128 + 128] for r in range(8)],
                    lax.broadcasted_iota(jnp.int32, (SUB, 128), 1),
                )
                for r in range(8):
                    i = block_i * 8 + r
                    here = done[i * SUB:(i + 1) * SUB, lanes]
                    shift = (row - eo_block[i]) * scale
                    denom = down + jnp.concatenate([shift, shift], axis=0)
                    guess = pl.reciprocal(denom, approx=True)
                    inverse = guess * (2.0 - denom * guess)
                    term = (here * (here - mirror[r]) + mirror[r] * mirror[r]) * inverse
                    acc[i, :, lanes] = acc[i, :, lanes] + (term[:8] + term[8:])

    def step_body(step, carry):
        split_done, old_left, old_right, old_weight = carry

        def arrivals(index):
            first = 0 if index == 0 else UPTO[index - 2]
            for slot, part, way, _source in HOPS[first:UPTO[index]]:
                event(slot, part, way)

        def before(index):
            arrivals(2 * index)
            for slot in READY[index]:
                for part in range(4):
                    sib_copy(slot, part, 1).wait_recv()
            if index == 0:
                for dy, dk in line:
                    eo_arrival(dy, dk).wait_recv()
                for block in range(3):
                    value = jnp.zeros((8, 128), jnp.float32)
                    for r in range(8):
                        value = jnp.where(lane // SUB == r, eo_block[block * 8 + r], value)
                    eo_lane[block] = value

        def choose(function, wanted):
            wanted = [index for index in range(len(UNITS)) if wanted(index)]
            for start in range(0, len(wanted), 4):
                some = wanted[start:start + 4]

                @pl.when((step >= some[0]) & (step <= some[-1]))
                def _():
                    for index in some:
                        pl.when(step == index)(functools.partial(function, index))

        choose(before, lambda index: READY[index] or UPTO[2 * index] > (UPTO[2 * index - 2] if index else 0))
        split_upto = jnp.int32(0)
        for index in range(len(UNITS)):
            if READY[index]:
                split_upto = split_upto + jnp.where(step >= index, jnp.int32(len(READY[index])), 0)

        def one_split(index, carry):
            split(index)
            return carry

        lax.fori_loop(split_done, split_upto, one_split, 0)

        left, right, weight = (pick(step, table) for table in tables)
        dot = functools.partial(lax.dot_general, dimension_numbers=contract, preferred_element_type=jnp.float32)
        wide = dot(both[left, :ROWS], both[right])
        narrow = dot(both[left, ROWS:], both[right, :ROWS])
        energies(old_left, old_right, old_weight)
        done[...] = wide[:, :ROWS] + wide[:, ROWS:] + narrow
        return split_upto, left, right, weight

    zero = jnp.int32(0)
    _, left, right, weight = lax.fori_loop(0, len(UNITS), step_body, (zero, zero, zero, zero))
    energies(left, right, weight)

    member = lax.broadcasted_iota(jnp.int32, (128, ROWS), 1) // SUB == lax.broadcasted_iota(jnp.int32, (128, ROWS), 0)
    group = member.astype(jnp.float32)
    summed = jnp.concatenate([jnp.sum(acc[...], axis=1), jnp.zeros((128 - OCC, ROWS), jnp.float32)], axis=0)
    exact = functools.partial(
        lax.dot_general, dimension_numbers=contract,
        precision=lax.Precision.HIGHEST, preferred_element_type=jnp.float32,
    )
    upper, lower = exact(summed, group), exact(group, summed)
    below = lax.broadcasted_iota(jnp.int32, (128, 128), 0) // 8 > lax.broadcasted_iota(jnp.int32, (128, 128), 1) // 8
    pairs = upper + jnp.where(below, lower, 0.0)

    rows_out[...] = jnp.zeros_like(rows_out)
    for owner in range(8):
        rows_out[owner, 0:3, :] = pairs[owner * 3:owner * 3 + 3, :]

    def red_copy(dy, dk):
        far = line_device(dy, dk)
        return pltpu.make_async_remote_copy(
            src_ref=rows_out.at[far[0]], dst_ref=rows_got.at[occ],
            send_sem=red_out.at[dy, dk], recv_sem=red_in.at[dy, dk],
            device_id=far, device_id_type=MESH,
        )

    def red_arrival(dy, dk):
        source = line_device((4 - dy) % 4, dk)
        return pltpu.make_async_remote_copy(
            src_ref=rows_out.at[occ], dst_ref=rows_got.at[source[0]],
            send_sem=red_out.at[dy, dk], recv_sem=red_in.at[dy, dk],
            device_id=source, device_id_type=MESH,
        )

    for dy, dk in line:
        red_copy(dy, dk).start()
    for slot, part, way, source in HOPS:
        sib_copy(slot, part, 0).wait_send()
        if way >= 0:
            hop_copy(slot, part, way, source).wait_send()
    rows_got[occ] = rows_out[occ]
    for dy, dk in line:
        red_arrival(dy, dk).wait_recv()
    value = functools.reduce(lambda p, q: p + q, [rows_got[owner] for owner in range(8)])

    place = x * 4 + z
    plane_got[place] = value
    plane = [(dx, dz) for dx in (2, 1, 3, 0) for dz in (2, 1, 3, 0) if (dx, dz) != (0, 0)]

    def plane_copy(dx, dz, to):
        far = device(xs[dx], y, zs[dz], core)
        return pltpu.make_async_remote_copy(
            src_ref=plane_got.at[place], dst_ref=plane_got.at[to],
            send_sem=plane_out.at[dx, dz], recv_sem=plane_in.at[dx, dz],
            device_id=far, device_id_type=MESH,
        )

    for dx, dz in plane:
        plane_copy(dx, dz, place).start()
    for slot, (source, way) in EPS_FROM.items():
        ev_copy(slot, way, source).wait_send()
    for dy, dk in line:
        row_copy(dy, dk).wait_send()
        eo_copy(dy, dk).wait_send()
        red_copy(dy, dk).wait_send()
    for dx, dz in plane:
        plane_copy(dx, dz, xs[(4 - dx) % 4] * 4 + zs[(4 - dz) % 4]).wait_recv()
    value = functools.reduce(lambda p, q: p + q, [plane_got[n] for n in range(16)])
    out_ref[...] = -value[:3, :OCC]
    for dx, dz in plane:
        plane_copy(dx, dz, place).wait_send()


def on_device(factors, eps_occ, eps_vir):
    f32, dma = jnp.float32, pltpu.SemaphoreType.DMA
    return pl.pallas_call(
        kernel,
        out_shape=jax.ShapeDtypeStruct((3, OCC), f32),
        in_specs=[
            pl.BlockSpec(memory_space=pltpu.SMEM),
            pl.BlockSpec(memory_space=pltpu.SMEM),
            pl.BlockSpec(memory_space=pl.ANY),
        ],
        out_specs=pl.BlockSpec(memory_space=pltpu.VMEM),
        scratch_shapes=[
            pltpu.VMEM((SLOTS, OCC, SUB, NAUX), f32),
            pltpu.VMEM((SLOTS, 2 * ROWS, NAUX), jnp.bfloat16),
            pltpu.VMEM((ROWS, ROWS), f32),
            pltpu.VMEM((OCC, 8, ROWS), f32),
            pltpu.VMEM((SLOTS, 24, 128), f32),
            pltpu.VMEM((OCC, 8, 128), f32),
            pltpu.VMEM((3, 8, 128), f32),
            pltpu.VMEM((8, 8, 128), f32), pltpu.VMEM((8, 8, 128), f32),
            pltpu.VMEM((16, 8, 128), f32),
            dma((SLOTS, 4)), dma((SLOTS, 4)),
            dma((SLOTS, 4)), dma((SLOTS, 4)),
            dma((4, 2)), dma((4, 2)),
            dma((SLOTS,)), dma((SLOTS,)),
            dma((4, 2)), dma((4, 2)),
            dma,
            dma((4, 2)), dma((4, 2)), dma((4, 4)), dma((4, 4)),
        ],
        compiler_params=pltpu.CompilerParams(
            collective_id=0, has_side_effects=True, vmem_limit_bytes=61 * 2**20
        ),
        cost_estimate=pl.CostEstimate(flops=45 * 10**9, bytes_accessed=2 * 10**6, transcendentals=0),
    )(eps_occ, eps_vir, factors)


def solution(mesh):
    placed = (P("occ", ("va", "vb"), None), P("occ"), P(("va", "vb")))
    return jax.shard_map(on_device, mesh=mesh, in_specs=placed, out_specs=P("occ", None), check_vma=False)
```

```python
import functools

import jax
import jax.numpy as jnp
from jax import lax
from jax.experimental import pallas as pl
from jax.experimental.pallas import tpu as pltpu
from jax.sharding import PartitionSpec as P

MESH = pl.DeviceIdType.MESH
STEPS = ((1, 0, 0), (3, 0, 0), (0, 1, 0), (0, 3, 0), (0, 0, 1), (0, 0, 3))
OCC, SUB, NAUX = 24, 16, 1408
ROWS = OCC * SUB

POINTS = ((0, 0, 0), (0, 0, 3), (3, 0, 0), (1, 0, 0), (3, 0, 1), (0, 1, 0), (0, 3, 3), (2, 0, 0), (2, 0, 1), (0, 3, 2), (0, 2, 0), (0, 2, 2))
HOPS = (
    (0, 0, -1, -1),
    (0, 1, -1, -1),
    (0, 3, -1, -1),
    (1, 0, 5, 0),
    (3, 0, 0, 0),
    (2, 0, 1, 0),
    (0, 2, -1, -1),
    (1, 1, 5, 0),
    (3, 1, 0, 0),
    (2, 1, 1, 0),
    (4, 0, 4, 2),
    (5, 0, 2, 0),
    (6, 0, 3, 1),
    (1, 3, 5, 0),
    (3, 3, 0, 0),
    (2, 3, 1, 0),
    (4, 1, 4, 2),
    (5, 1, 2, 0),
    (6, 1, 3, 1),
    (1, 2, 5, 0),
    (7, 0, 0, 3),
    (2, 2, 1, 0),
    (4, 3, 4, 2),
    (5, 3, 2, 0),
    (6, 3, 3, 1),
    (9, 0, 5, 6),
    (3, 2, 0, 0),
    (7, 1, 1, 2),
    (4, 2, 4, 2),
    (5, 2, 2, 0),
    (6, 2, 3, 1),
    (9, 1, 5, 6),
    (7, 3, 0, 3),
    (8, 0, 1, 4),
    (8, 1, 4, 7),
    (10, 0, 2, 5),
    (11, 0, 3, 9),
    (9, 3, 5, 6),
    (7, 2, 0, 3),
    (8, 2, 1, 4),
    (8, 3, 4, 7),
    (10, 1, 2, 5),
    (11, 1, 3, 9),
    (9, 2, 5, 6),
    (10, 3, 2, 5),
    (11, 3, 3, 9),
    (10, 2, 2, 5),
    (11, 2, 3, 9),
)
UPTO = (
    22, 23, 23, 28, 29, 29, 31, 34, 34, 35, 37, 40,
    40, 41, 43, 44, 44, 44, 44, 46, 46, 46, 46, 46,
    48, 48, 48, 48, 48, 48, 48, 48, 48, 48, 48, 48,
)
UNITS = (
    ((0, 0, 1), (1, 0, 2)),
    ((2, 1, 2), (0, 2, 2)),
    ((3, 2, 1), (3, 1, 2)),
    ((3, 4, 2), (1, 4, 2)),
    ((2, 5, 2), (1, 5, 2)),
    ((3, 5, 2), (4, 5, 2)),
    ((5, 0, 2), (6, 5, 2)),
    ((2, 6, 2), (3, 6, 2)),
    ((4, 6, 2), (7, 5, 2)),
    ((6, 7, 2), (8, 5, 2)),
    ((1, 8, 1), (8, 6, 2)),
    ((4, 9, 2), (9, 5, 1)),
    ((9, 0, 2), (3, 9, 2)),
    ((4, 10, 2), (10, 6, 2)),
    ((3, 10, 2), (7, 10, 1)),
    ((10, 8, 2), (10, 0, 1)),
    ((11, 7, 1), (11, 3, 2)),
    ((11, 10, 1), (11, 4, 2)),
)

SLOTS = len(POINTS)
CHILDREN = {}
for _slot, _part, _way, _from in HOPS:
    if _way >= 0:
        CHILDREN.setdefault((_from, _part), []).append((_slot, _way))
EPS_FROM = {slot: (source, way) for slot, part, way, source in HOPS if part == 0 and way >= 0}
READY = []
_seen = set()
for _pair in UNITS:
    _new = sorted({slot for unit in _pair for slot in unit[:2]} - _seen)
    _seen.update(_new)
    READY.append(_new)


PACK = 7


def words(core, field):
    out = []
    for start in range(0, len(UNITS), PACK):
        pair = [sum(u[side][field] << (4 * n) for n, u in enumerate(UNITS[start:start + PACK])) for side in range(2)]
        out.append(jnp.where(core == 0, jnp.int32(pair[0]), jnp.int32(pair[1])))
    return out


def pick(step, table):
    word = table[-1]
    for n in range(len(table) - 1, 0, -1):
        word = jnp.where(step < n * PACK, table[n - 1], word)
    return lax.shift_right_logical(word, 4 * lax.rem(step, PACK)) & 15


def swap_pairs(rows, lane):
    rows = list(rows)
    for bit in (4, 2, 1):
        low = (lane // (16 * bit)) % 2 == 0
        for r in range(8):
            if r & bit:
                continue
            first, second = rows[r], rows[r + bit]
            rows[r] = jnp.where(low, first, pltpu.roll(second, 16 * bit, 1))
            rows[r + bit] = jnp.where(low, pltpu.roll(first, 128 - 16 * bit, 1), second)
    return rows


def kernel(
    eps_occ, eps_vir, b_ref, out_ref,
    held, both, done, acc, evs, eo_block, eo_lane,
    rows_out, rows_got, plane_got,
    hop_out, hop_in, sib_out, sib_in, row_out, row_in, ev_out, ev_in, eo_out, eo_in, own_sem,
    red_out, red_in, plane_out, plane_in,
):
    occ, va, vb = lax.axis_index("occ"), lax.axis_index("va"), lax.axis_index("vb")
    y, core = occ >> 1, occ & 1
    x, z = vb >> 1, (vb & 1) * 2 + va
    other = 1 - core

    def device(cx, cy, cz, ck):
        return (cy * 2 + ck, cz & 1, cx * 2 + (cz >> 1))

    xs, ys, zs = ([(place + d) & 3 for d in range(4)] for place in (x, y, z))
    sibling = device(x, y, z, other)
    near = [device(xs[(4 - dx) % 4], ys[(4 - dy) % 4], zs[(4 - dz) % 4], core) for dx, dy, dz in STEPS]
    quarter = [place * 6 for place in ys]
    half = (pl.multiple_of(core * 8, 8), pl.multiple_of(other * 8, 8))
    line = [(dy, dk) for dy in range(4) for dk in range(2) if (dy, dk) != (0, 0)]
    line_at = {(dy, dk): device(x, ys[dy], z, other if dk else core) for dy in range(4) for dk in range(2)}

    def to_step(way):
        return near[way]

    def line_device(dy, dk):
        return line_at[dy, dk]

    barrier = pltpu.get_barrier_semaphore()
    partners = [line_device(dy, dk) for dy, dk in line]
    partners += [device(xs[dx], y, zs[dz], core) for dx in range(4) for dz in range(4) if (dx, dz) != (0, 0)]
    for partner in partners:
        pl.semaphore_signal(barrier, inc=1, device_id=partner, device_id_type=MESH)
    pl.semaphore_wait(barrier, len(partners))

    def piece(slot, part, side):
        start = quarter[(POINTS[slot][1] + part) % 4]
        return held.at[slot, pl.ds(start, 6), pl.ds(half[side], 8), :]

    def row_copy(dy, dk):
        far = line_device(dy, dk)
        far_occ = far[0]
        return pltpu.make_async_remote_copy(
            src_ref=b_ref.at[:, pl.ds(pl.multiple_of(far_occ * 8, 8), 8), :],
            dst_ref=held.at[0, pl.ds(occ * 3, 3), pl.ds(half[dk], 8), :],
            send_sem=row_out.at[dy, dk], recv_sem=row_in.at[dy, dk],
            device_id=far, device_id_type=MESH,
        )

    def row_arrival(dy, dk):
        source = line_device((4 - dy) % 4, dk)
        place = held.at[0, pl.ds(source[0] * 3, 3), pl.ds(half[0], 8), :]
        return pltpu.make_async_remote_copy(
            src_ref=place, dst_ref=place, send_sem=row_out.at[dy, dk], recv_sem=row_in.at[dy, dk],
            device_id=source, device_id_type=MESH,
        )

    def sib_copy(slot, part, side):
        return pltpu.make_async_remote_copy(
            src_ref=piece(slot, part, side), dst_ref=piece(slot, part, side),
            send_sem=sib_out.at[slot, part], recv_sem=sib_in.at[slot, part],
            device_id=sibling, device_id_type=MESH,
        )

    def hop_copy(slot, part, way, source):
        return pltpu.make_async_remote_copy(
            src_ref=piece(source, part, 0),
            dst_ref=held.at[
                slot,
                pl.ds(quarter[(POINTS[source][1] + part) % 4], 6),
                pl.ds(half[0], 8),
                :,
            ],
            send_sem=hop_out.at[slot, part], recv_sem=hop_in.at[slot, part],
            device_id=to_step(way), device_id_type=MESH,
        )

    def hop_arrival(slot, part, way):
        return pltpu.make_async_remote_copy(
            src_ref=piece(slot, part, 0), dst_ref=piece(slot, part, 0),
            send_sem=hop_out.at[slot, part], recv_sem=hop_in.at[slot, part],
            device_id=to_step(way), device_id_type=MESH,
        )

    def ev_copy(slot, way, source):
        return pltpu.make_async_remote_copy(
            src_ref=evs.at[source], dst_ref=evs.at[slot], send_sem=ev_out.at[slot], recv_sem=ev_in.at[slot],
            device_id=to_step(way), device_id_type=MESH,
        )

    def eo_copy(dy, dk):
        return pltpu.make_async_remote_copy(
            src_ref=eo_block.at[pl.ds(occ * 3, 3)], dst_ref=eo_block.at[pl.ds(occ * 3, 3)],
            send_sem=eo_out.at[dy, dk], recv_sem=eo_in.at[dy, dk],
            device_id=line_device(dy, dk), device_id_type=MESH,
        )

    def eo_arrival(dy, dk):
        source = line_device((4 - dy) % 4, dk)
        place = eo_block.at[pl.ds(source[0] * 3, 3)]
        return pltpu.make_async_remote_copy(
            src_ref=place, dst_ref=place, send_sem=eo_out.at[dy, dk], recv_sem=eo_in.at[dy, dk],
            device_id=source, device_id_type=MESH,
        )

    own = pltpu.make_async_copy(
        b_ref.at[:, pl.ds(pl.multiple_of(occ * 8, 8), 8), :],
        held.at[0, pl.ds(occ * 3, 3), pl.ds(half[0], 8), :],
        own_sem,
    )
    row_copy(0, 1).start()
    own.start()
    for dy, dk in line[1:]:
        if dy != 2:
            row_copy(dy, dk).start()
    for dk in range(2):
        row_copy(2, dk).start()

    lane = lax.broadcasted_iota(jnp.int32, (8, 128), 1)
    sub16 = lax.broadcasted_iota(jnp.int32, (16, 128), 0)
    down = jnp.zeros((16, 128), jnp.float32)
    across = jnp.zeros((8, 128), jnp.float32)
    for a in range(SUB):
        value = eps_vir[y * SUB + a]
        down = jnp.where(sub16 == a, value, down)
        across = jnp.where(lane % SUB == a, value, across)
    evs[0, :16, :] = down
    evs[0, 16:, :] = across
    for r in range(3):
        eo_block[occ * 3 + r] = jnp.full((8, 128), eps_occ[r], jnp.float32)
    for slot, (source, way) in EPS_FROM.items():
        if source == 0:
            ev_copy(slot, way, source).start()
    for dy, dk in line:
        eo_copy(dy, dk).start()
    acc[...] = jnp.zeros_like(acc)
    done[...] = jnp.zeros_like(done)

    def event(slot, part, way):
        if slot == 0:
            dy = (4 - part) % 4
            for dk in range(2):
                if (dy, dk) == (0, 0):
                    own.wait()
                else:
                    row_arrival(dy, dk).wait_recv()
        else:
            hop_arrival(slot, part, way).wait_recv()
        for child, child_way in CHILDREN.get((slot, part), []):
            hop_copy(child, part, child_way, slot).start()
        sib_copy(slot, part, 0).start()
        if part == 0 and slot:
            source, ev_way = EPS_FROM[slot]
            ev_copy(slot, ev_way, source).wait_recv()
            for child, (child_from, child_way) in EPS_FROM.items():
                if child_from == slot:
                    ev_copy(child, child_way, slot).start()

    def split(slot):
        def rows(i, carry):
            value = held[slot, i]
            top = value.astype(jnp.bfloat16)
            at = pl.ds(pl.multiple_of(i * SUB, SUB), SUB)
            both[slot, at, :] = top
            both[slot, pl.ds(pl.multiple_of(ROWS + i * SUB, SUB), SUB), :] = (value - top.astype(jnp.float32)).astype(jnp.bfloat16)
            return carry
        lax.fori_loop(0, OCC, rows, 0)

    contract = (((1,), (1,)), ((), ()))

    tables = [words(core, field) for field in range(3)]

    def energies(left, right, weight):
        scale = jnp.where(weight == 2, jnp.float32(0.5), jnp.float32(1.0))
        down = evs[left, :16, :] * scale
        across = evs[right, 16:, :]
        for block_j in range(3):
            lanes = pl.ds(block_j * 128, 128)
            row = across - eo_lane[block_j]
            for block_i in range(block_j + 1):
                mirror = swap_pairs(
                    [done[(block_j * 8 + r) * SUB:(block_j * 8 + r + 1) * SUB, block_i * 128:block_i * 128 + 128] for r in range(8)],
                    lax.broadcasted_iota(jnp.int32, (SUB, 128), 1),
                )
                for r in range(8):
                    i = block_i * 8 + r
                    here = done[i * SUB:(i + 1) * SUB, lanes]
                    shift = (row - eo_block[i]) * scale
                    denom = down + jnp.concatenate([shift, shift], axis=0)
                    guess = pl.reciprocal(denom, approx=True)
                    inverse = guess * (2.0 - denom * guess)
                    term = (here * (here - mirror[r]) + mirror[r] * mirror[r]) * inverse
                    acc[i, :, lanes] = acc[i, :, lanes] + (term[:8] + term[8:])

    def step_body(step, carry):
        split_done, old_left, old_right, old_weight = carry

        def arrivals(index):
            first = 0 if index == 0 else UPTO[index - 2]
            for slot, part, way, _source in HOPS[first:UPTO[index]]:
                event(slot, part, way)

        def before(index):
            arrivals(2 * index)
            for slot in READY[index]:
                for part in range(4):
                    sib_copy(slot, part, 1).wait_recv()
            if index == 0:
                for dy, dk in line:
                    eo_arrival(dy, dk).wait_recv()
                for block in range(3):
                    value = jnp.zeros((8, 128), jnp.float32)
                    for r in range(8):
                        value = jnp.where(lane // SUB == r, eo_block[block * 8 + r], value)
                    eo_lane[block] = value

        def choose(function, wanted):
            wanted = [index for index in range(len(UNITS)) if wanted(index)]
            for start in range(0, len(wanted), 4):
                some = wanted[start:start + 4]

                @pl.when((step >= some[0]) & (step <= some[-1]))
                def _():
                    for index in some:
                        pl.when(step == index)(functools.partial(function, index))

        choose(before, lambda index: READY[index] or UPTO[2 * index] > (UPTO[2 * index - 2] if index else 0))
        split_upto = jnp.int32(0)
        for index in range(len(UNITS)):
            if READY[index]:
                split_upto = split_upto + jnp.where(step >= index, jnp.int32(len(READY[index])), 0)

        def one_split(index, carry):
            split(index)
            return carry

        lax.fori_loop(split_done, split_upto, one_split, 0)

        left, right, weight = (pick(step, table) for table in tables)
        dot = functools.partial(lax.dot_general, dimension_numbers=contract, preferred_element_type=jnp.float32)
        wide = dot(both[left, :ROWS], both[right])
        narrow = dot(both[left, ROWS:], both[right, :ROWS])
        energies(old_left, old_right, old_weight)
        done[...] = wide[:, :ROWS] + wide[:, ROWS:] + narrow
        return split_upto, left, right, weight

    zero = jnp.int32(0)
    _, left, right, weight = lax.fori_loop(0, len(UNITS), step_body, (zero, zero, zero, zero))
    energies(left, right, weight)

    member = lax.broadcasted_iota(jnp.int32, (128, ROWS), 1) // SUB == lax.broadcasted_iota(jnp.int32, (128, ROWS), 0)
    group = member.astype(jnp.float32)
    summed = jnp.concatenate([jnp.sum(acc[...], axis=1), jnp.zeros((128 - OCC, ROWS), jnp.float32)], axis=0)
    exact = functools.partial(
        lax.dot_general, dimension_numbers=contract,
        precision=lax.Precision.HIGHEST, preferred_element_type=jnp.float32,
    )
    upper, lower = exact(summed, group), exact(group, summed)
    below = lax.broadcasted_iota(jnp.int32, (128, 128), 0) // 8 > lax.broadcasted_iota(jnp.int32, (128, 128), 1) // 8
    pairs = upper + jnp.where(below, lower, 0.0)

    rows_out[...] = jnp.zeros_like(rows_out)
    for owner in range(8):
        rows_out[owner, 0:3, :] = pairs[owner * 3:owner * 3 + 3, :]

    def red_copy(dy, dk):
        far = line_device(dy, dk)
        return pltpu.make_async_remote_copy(
            src_ref=rows_out.at[far[0]], dst_ref=rows_got.at[occ],
            send_sem=red_out.at[dy, dk], recv_sem=red_in.at[dy, dk],
            device_id=far, device_id_type=MESH,
        )

    def red_arrival(dy, dk):
        source = line_device((4 - dy) % 4, dk)
        return pltpu.make_async_remote_copy(
            src_ref=rows_out.at[occ], dst_ref=rows_got.at[source[0]],
            send_sem=red_out.at[dy, dk], recv_sem=red_in.at[dy, dk],
            device_id=source, device_id_type=MESH,
        )

    for dy, dk in line:
        red_copy(dy, dk).start()
    rows_got[occ] = rows_out[occ]
    for dy, dk in line:
        red_arrival(dy, dk).wait_recv()
    value = functools.reduce(lambda p, q: p + q, [rows_got[owner] for owner in range(8)])

    place = x * 4 + z
    plane_got[place] = value
    plane = [(dx, dz) for dx in (2, 1, 3, 0) for dz in (2, 1, 3, 0) if (dx, dz) != (0, 0)]

    def plane_copy(dx, dz, to):
        far = device(xs[dx], y, zs[dz], core)
        return pltpu.make_async_remote_copy(
            src_ref=plane_got.at[place], dst_ref=plane_got.at[to],
            send_sem=plane_out.at[dx, dz], recv_sem=plane_in.at[dx, dz],
            device_id=far, device_id_type=MESH,
        )

    for dx, dz in plane:
        plane_copy(dx, dz, place).start()
    for slot, part, way, source in HOPS:
        sib_copy(slot, part, 0).wait_send()
        if way >= 0:
            hop_copy(slot, part, way, source).wait_send()
    for slot, (source, way) in EPS_FROM.items():
        ev_copy(slot, way, source).wait_send()
    for dy, dk in line:
        row_copy(dy, dk).wait_send()
        eo_copy(dy, dk).wait_send()
        red_copy(dy, dk).wait_send()
    for dx, dz in plane:
        plane_copy(dx, dz, xs[(4 - dx) % 4] * 4 + zs[(4 - dz) % 4]).wait_recv()
    value = functools.reduce(lambda p, q: p + q, [plane_got[n] for n in range(16)])
    out_ref[...] = -value[:3, :OCC]
    for dx, dz in plane:
        plane_copy(dx, dz, place).wait_send()


def on_device(factors, eps_occ, eps_vir):
    f32, dma = jnp.float32, pltpu.SemaphoreType.DMA
    return pl.pallas_call(
        kernel,
        out_shape=jax.ShapeDtypeStruct((3, OCC), f32),
        in_specs=[
            pl.BlockSpec(memory_space=pltpu.SMEM),
            pl.BlockSpec(memory_space=pltpu.SMEM),
            pl.BlockSpec(memory_space=pl.ANY),
        ],
        out_specs=pl.BlockSpec(memory_space=pltpu.VMEM),
        scratch_shapes=[
            pltpu.VMEM((SLOTS, OCC, SUB, NAUX), f32),
            pltpu.VMEM((SLOTS, 2 * ROWS, NAUX), jnp.bfloat16),
            pltpu.VMEM((ROWS, ROWS), f32),
            pltpu.VMEM((OCC, 8, ROWS), f32),
            pltpu.VMEM((SLOTS, 24, 128), f32),
            pltpu.VMEM((OCC, 8, 128), f32),
            pltpu.VMEM((3, 8, 128), f32),
            pltpu.VMEM((8, 8, 128), f32), pltpu.VMEM((8, 8, 128), f32),
            pltpu.VMEM((16, 8, 128), f32),
            dma((SLOTS, 4)), dma((SLOTS, 4)),
            dma((SLOTS, 4)), dma((SLOTS, 4)),
            dma((4, 2)), dma((4, 2)),
            dma((SLOTS,)), dma((SLOTS,)),
            dma((4, 2)), dma((4, 2)),
            dma,
            dma((4, 2)), dma((4, 2)), dma((4, 4)), dma((4, 4)),
        ],
        compiler_params=pltpu.CompilerParams(
            collective_id=0, has_side_effects=True, vmem_limit_bytes=61 * 2**20
        ),
        cost_estimate=pl.CostEstimate(flops=45 * 10**9, bytes_accessed=2 * 10**6, transcendentals=0),
    )(eps_occ, eps_vir, factors)


def solution(mesh):
    placed = (P("occ", ("va", "vb"), None), P("occ"), P(("va", "vb")))
    return jax.shard_map(on_device, mesh=mesh, in_specs=placed, out_specs=P("occ", None), check_vma=False)
```
